128 devices in a mesh: dp: 16 (over x, z), col: 8 (over y, core).
Axes of the slice: x: 4, y: 4, z: 4, core: 2. Of those that a mesh axis runs over, the one named last changes fastest.
Arguments:
- tokens: bfloat16 [4096, 5120], P('dp', 'col'), may hold values from -72 to 72
- query_weight: bfloat16 [5120, 5120], P('dp', 'col'), may hold values from -0.078125 to 0.078125
- key_weight: bfloat16 [5120, 5120], P('dp', 'col'), may hold values from -0.078125 to 0.078125
- old_maps: bfloat16 [960, 16, 256, 256], P(None, 'dp', 'col'), may hold values from 9.9658966e-05 to 0.5
- pair_weight: bfloat16 [1000, 128], replicated, may hold values from -0.75 to 0.75
- pair_bias: float32 [128], replicated, may hold values from -1.5 to 1.5
- norm_gain: float32 [128], replicated, may hold values from 0.25 to 1.75
- norm_bias: float32 [128], replicated, may hold values from -1.5 to 1.5
- hidden_weight: bfloat16 [128, 512], replicated, may hold values from -0.5 to 0.5
- hidden_bias: float32 [512], replicated, may hold values from -1.5 to 1.5
- out_weight: bfloat16 [512, 128], replicated, may hold values from -0.25 to 0.25
- out_bias: float32 [128], replicated, may hold values from -1.5 to 1.5
- chain_starts: int32 [16, 8], P('dp'), may hold values from 0 to 244, as said below
- chain_lengths: int32 [16, 8], P('dp'), may hold values from 12 to 172
- chain_groups: int32 [16, 8], P('dp'), may hold values from 0 to 7, as said below
- tile_owner: int32 [16, 8, 8], P('dp', 'col'), may hold values from -1 to 15, as said below
Outputs:
- pair_tiles: bfloat16 [16, 16, 8, 1024, 128], P('dp', None, 'col')
The draws below stay inside these ranges and needn't reach their ends.
Inputs may be any that keep to these rules, and one draw needn't show every extreme that they name: `chain_starts`: in each bin the chains do not intersect, lie in increasing order and end exactly at token 256; between two chains at most 4 tokens belong to no chain. `chain_groups`: complex numbers start at 0 in each bin and never fall along the chains; only tokens of one complex attend to each other. `tile_owner`: A tile's owner is -1 exactly when the tile holds no pair of two tokens of one complex. Within one bin and key block, tiles have distinct owners; for each key block one owner receives a tile from every bin, so an owner receives at most 16 tiles of a key block.
All inputs are finite; a program needn't handle non-finite values.
Results may differ from the reference program's by a relative error of at most 0.012.
Values may be sent and summed in bfloat16 or wider, within the bound.
No kernel may reach another device: no remote copies, remote signals or barrier semaphores. Data moves between devices by JAX's collectives and lax.ppermute only.
A program may use at most 128 MiB of HBM per device.

```python
import math
import jax
import jax.numpy as jnp
from jax import lax

D = 5120
HEADS = 40
HEAD = 128
CH_OLD = 960
PAIR = 128
PAIR_HID = 512
CHAINS_PER_BIN = 8
ROWT = 8
TOKENS_PER_BIN = 256
TOKENS = 4096
TILE = 1024
N_DP = 16
N_COL = 8


def chain_layout(key):
    folded = jax.random.fold_in(key, 11)
    random_seeds = jax.random.split(folded, 6)
    lower_limit = TOKENS_PER_BIN * 3 // 64
    upper_limit = TOKENS_PER_BIN * 7 // 64 + 1
    bin_rows = jnp.arange(N_DP, dtype=jnp.int32)[:, None]
    lead_cols = jnp.arange(CHAINS_PER_BIN - 1, dtype=jnp.int32)[None, :]
    leading_chain = jax.random.randint(random_seeds[0], (N_DP, CHAINS_PER_BIN - 1), lower_limit, upper_limit, dtype=jnp.int32)
    leading_chain = jnp.where(bin_rows == 1, lower_limit, leading_chain)
    leading_chain = jnp.where((bin_rows == 0) & (lead_cols == CHAINS_PER_BIN - 2), lower_limit, leading_chain).astype(jnp.int32)
    break_spacing = jax.random.randint(random_seeds[1], (N_DP, CHAINS_PER_BIN), 0, TOKENS_PER_BIN // 64 + 1, dtype=jnp.int32)
    break_spacing = jnp.where(bin_rows == 1, 0, break_spacing).astype(jnp.int32)
    closing = TOKENS_PER_BIN - jnp.sum(leading_chain, axis=1, keepdims=True) - jnp.sum(break_spacing, axis=1, keepdims=True)
    lengths = jnp.concatenate([leading_chain, closing], axis=1).astype(jnp.int32)
    lengths = jnp.where(bin_rows == 0, jnp.roll(lengths, 1, axis=1), lengths).astype(jnp.int32)
    starts = (jnp.cumsum(lengths + break_spacing, axis=1) - lengths).astype(jnp.int32)
    break_probability = jax.random.randint(random_seeds[2], (N_DP, 1), 0, 4, dtype=jnp.int32)
    break_probability = jnp.where(bin_rows == 0, 4, break_probability)
    chain_boundaries = (jax.random.randint(random_seeds[3], (N_DP, CHAINS_PER_BIN - 1), 0, 4, dtype=jnp.int32) < break_probability).astype(jnp.int32)
    groups = jnp.concatenate([jnp.zeros((N_DP, 1), jnp.int32), jnp.cumsum(chain_boundaries, axis=1).astype(jnp.int32)], axis=1)
    places = jnp.arange(TOKENS_PER_BIN, dtype=jnp.int32)
    member = (places[None, :, None] >= starts[:, None, :]) & (places[None, :, None] < (starts + lengths)[:, None, :])
    inside = jnp.any(member, axis=2)
    group_ids = jnp.sum(jnp.where(member, groups[:, None, :], 0), axis=2)
    same_group = inside[:, :, None] & inside[:, None, :] & (group_ids[:, :, None] == group_ids[:, None, :])
    live_tiles = jnp.any(same_group.reshape(N_DP, N_COL, TOKENS_PER_BIN // N_COL, ROWT, TOKENS_PER_BIN // ROWT), axis=(2, 4))
    tile_rank = jnp.cumsum(live_tiles.astype(jnp.int32), axis=2) - 1
    anchor = jax.random.randint(random_seeds[4], (N_COL,), 0, N_DP, dtype=jnp.int32)
    others = N_DP - 1
    order_keys = jax.random.randint(random_seeds[5], (N_DP, N_COL, others), 0, 4096, dtype=jnp.int32) * others + jnp.arange(others, dtype=jnp.int32)
    shuffled = jnp.argsort(order_keys, axis=2, stable=True).astype(jnp.int32)
    picked = jnp.take_along_axis(shuffled, jnp.clip(tile_rank - 1, 0, others - 1), axis=2)
    owners = jnp.where(tile_rank == 0, anchor[None, :, None], (anchor[None, :, None] + 1 + picked) % N_DP)
    owners = jnp.where(live_tiles, owners, -1).astype(jnp.int32)
    return (starts, lengths, groups, owners)


def draw_chain_starts(key, part):
    return chain_layout(key)[0]


def draw_chain_lengths(key, part):
    return chain_layout(key)[1]


def draw_chain_groups(key, part):
    return chain_layout(key)[2]


def draw_tile_owner(key, part):
    return chain_layout(key)[3]


def draw_tokens(key, part):
    random_seeds = jax.random.split(jax.random.fold_in(key, 3), 1)
    normals = jnp.clip(jax.random.normal(random_seeds[0], (TOKENS, D), jnp.float32), -6.0, 6.0)
    return normals.astype(jnp.bfloat16)


def block_scale(rng, dims, cuts, low, high):
    def one(position, shards_of):
        draws = jax.random.uniform(jax.random.fold_in(jax.random.fold_in(rng, 6), position), (shards_of,), jnp.float32, low / len(cuts), high / len(cuts))
        return jnp.repeat(jnp.exp(draws), dims[position] // shards_of).reshape((-1,) + (1,) * (len(dims) - position - 1))

    factor_of = one(*cuts[0])
    for cut in cuts[1:]:
        factor_of = factor_of * one(*cut)
    return factor_of


def scatter_about(key, shape, scale, limit, pieces=(), kind=jnp.bfloat16):
    drawn = jax.random.normal(key, shape, jnp.float32) * scale
    if len(pieces) > 0:
        drawn = block_scale(key, shape, pieces, -0.22, 0.18) * drawn
    return jnp.clip(drawn, min=-limit, max=limit).astype(kind)


def setup_inputs(seed: int = 0) -> dict:
    splits = jax.random.split(jax.random.key(seed), 17)
    tokens = draw_tokens(jax.random.fold_in(splits[16], 71), 0)
    query_weight = scatter_about(splits[1], (D, D), D ** -0.5, 0.078125, ((0, 16), (1, 8)))
    key_weight = scatter_about(splits[2], (D, D), D ** -0.5, 0.078125, ((0, 16), (1, 8)))
    old_maps = jnp.clip(jnp.exp(math.log(0.5) - 8.520609 * jax.random.uniform(splits[3], (CH_OLD, N_DP, TOKENS_PER_BIN, TOKENS_PER_BIN), jnp.float32) ** block_scale(splits[3], (CH_OLD, N_DP, TOKENS_PER_BIN, TOKENS_PER_BIN), ((1, 16), (2, 8)), -0.2, 0.2)), 9.965896606445312e-05, 0.5).astype(jnp.bfloat16)
    pair_weight = scatter_about(splits[4], (CH_OLD + HEADS, PAIR), 64 ** -0.5, 0.75)
    pair_bias = scatter_about(splits[5], (PAIR,), 0.3, 1.5, (), jnp.float32)
    norm_gain = jnp.clip(1.0 + 0.15 * jax.random.normal(splits[6], (PAIR,), jnp.float32), 0.25, 1.75)
    norm_bias = scatter_about(splits[7], (PAIR,), 0.3, 1.5, (), jnp.float32)
    hidden_weight = scatter_about(splits[8], (PAIR, PAIR_HID), PAIR ** -0.5, 0.5)
    hidden_bias = scatter_about(splits[9], (PAIR_HID,), 0.3, 1.5, (), jnp.float32)
    out_weight = scatter_about(splits[10], (PAIR_HID, PAIR), PAIR_HID ** -0.5, 0.25)
    out_bias = scatter_about(splits[11], (PAIR,), 0.3, 1.5, (), jnp.float32)
    chain_starts = draw_chain_starts(jax.random.fold_in(splits[16], 71), 0)
    chain_lengths = draw_chain_lengths(jax.random.fold_in(splits[16], 71), 0)
    chain_groups = draw_chain_groups(jax.random.fold_in(splits[16], 71), 0)
    tile_owner = draw_tile_owner(jax.random.fold_in(splits[16], 71), 0)
    return dict(tokens=tokens, query_weight=query_weight, key_weight=key_weight, old_maps=old_maps, pair_weight=pair_weight, pair_bias=pair_bias, norm_gain=norm_gain, norm_bias=norm_bias, hidden_weight=hidden_weight, hidden_bias=hidden_bias, out_weight=out_weight, out_bias=out_bias, chain_starts=chain_starts, chain_lengths=chain_lengths, chain_groups=chain_groups, tile_owner=tile_owner)


def chain_tokens(starts, lengths, groups, token_count):
    places = jnp.arange(token_count, dtype=jnp.int32)
    member = (places[:, None] >= starts[None, :]) & (places[:, None] < (starts + lengths)[None, :])
    inside = jnp.any(member, axis=1)
    group_ids = lax.optimization_barrier(jnp.sum(jnp.where(member, groups[None, :], 0), axis=1)).astype(jnp.int32)
    offset = lax.optimization_barrier(jnp.sum(jnp.where(member, places[:, None] - starts[None, :], 0), axis=1))
    return (inside, group_ids, offset.astype(jnp.float32))

def rotate(values, offset):
    half_width = values.shape[-1] // 2
    frequency = jnp.exp(jnp.arange(half_width).astype(jnp.float32) * (-2.0 * math.log(10000.0) / values.shape[-1]))
    angles = offset[:, None] * frequency[None, :]
    cosine = jnp.cos(angles)[:, None, :]
    sine_table = jnp.sin(angles)[:, None, :]
    former = values[..., :half_width]
    latter = values[..., half_width:]
    return jnp.concatenate([former * cosine - latter * sine_table, latter * cosine + former * sine_table], axis=-1)

def head_maps(queries, key_rows, allowed):
    scores = jnp.einsum('jhd,ihd->hji', key_rows.astype(jnp.float32), queries.astype(jnp.float32)) / math.sqrt(queries.shape[-1])
    masked = jnp.where(allowed[None], scores, -jnp.inf)
    largest = lax.optimization_barrier(jnp.max(masked, axis=1, keepdims=True))
    powers = jnp.exp(masked - largest)
    return (powers / lax.optimization_barrier(jnp.sum(powers, axis=1, keepdims=True))).astype(jnp.bfloat16)

def refine(pair_rows, valid, norm_gain, norm_bias, hidden_weight, hidden_bias, out_weight, out_bias):
    values = pair_rows.astype(jnp.float32)
    average = lax.optimization_barrier(jnp.mean(values, axis=-1, keepdims=True))
    centred = values - average
    spread = lax.optimization_barrier(jnp.mean(centred * centred, axis=-1, keepdims=True))
    normed = (centred * lax.rsqrt(spread + 1e-05) * norm_gain + norm_bias).astype(jnp.bfloat16)
    hidden = jnp.maximum(jnp.dot(normed, hidden_weight, preferred_element_type=jnp.float32) + hidden_bias, 0.0).astype(jnp.bfloat16)
    update = jnp.dot(hidden, out_weight, preferred_element_type=jnp.float32) + out_bias
    return (valid[:, None] * (values + update)).astype(jnp.bfloat16)

def reference(tokens, query_weight, key_weight, old_maps, pair_weight, pair_bias, norm_gain, norm_bias, hidden_weight, hidden_bias, out_weight, out_bias, chain_starts, chain_lengths, chain_groups, tile_owner):

    def one_bin(bin_index):
        bin_rows = lax.dynamic_slice_in_dim(tokens, (bin_index * TOKENS_PER_BIN).astype(jnp.int32), TOKENS_PER_BIN, 0)
        inside, group_ids, offset = chain_tokens(chain_starts[bin_index], chain_lengths[bin_index], chain_groups[bin_index], TOKENS_PER_BIN)
        queries = jnp.dot(bin_rows, query_weight, preferred_element_type=jnp.float32).reshape(TOKENS_PER_BIN, HEADS, HEAD)
        key_rows = jnp.dot(bin_rows, key_weight, preferred_element_type=jnp.float32).reshape(TOKENS_PER_BIN, HEADS, HEAD)
        queries = rotate(queries, offset).astype(jnp.bfloat16)
        key_rows = rotate(key_rows, offset).astype(jnp.bfloat16)
        same_group = inside[:, None] & inside[None, :] & (group_ids[:, None] == group_ids[None, :])
        allowed = same_group | jnp.eye(TOKENS_PER_BIN, dtype=bool)
        prob_maps = head_maps(queries, key_rows, allowed)
        earlier = lax.dynamic_index_in_dim(old_maps, bin_index, 1, keepdims=False).reshape(CH_OLD, TOKENS_PER_BIN * TOKENS_PER_BIN)
        pair_rows = jnp.dot(earlier.T, pair_weight[:CH_OLD], preferred_element_type=jnp.float32)
        pair_rows = pair_rows + jnp.dot(prob_maps.reshape(HEADS, TOKENS_PER_BIN * TOKENS_PER_BIN).T, pair_weight[CH_OLD:], preferred_element_type=jnp.float32)
        pair_rows = (pair_rows + pair_bias).astype(jnp.bfloat16)
        refined = refine(pair_rows, same_group.reshape(-1).astype(jnp.float32), norm_gain, norm_bias, hidden_weight, hidden_bias, out_weight, out_bias)
        blocks = refined.reshape(N_COL, TOKENS_PER_BIN // N_COL, ROWT, TOKENS_PER_BIN // ROWT, PAIR).astype(jnp.float32)
        owners = tile_owner[bin_index]
        select = (owners[None] == jnp.arange(N_DP, dtype=jnp.int32)[:, None, None]).astype(jnp.float32)
        placed = jnp.einsum('ocr,cjrip->ocjip', select, blocks)
        return placed.reshape(N_DP, N_COL, TILE, PAIR).astype(jnp.bfloat16)
    per_bin = lax.map(one_bin, jnp.arange(N_DP, dtype=jnp.int32))
    return jnp.swapaxes(per_bin, 0, 1)
```

```python
import math

import jax
import jax.numpy as jnp
from jax import lax
from jax.experimental import pallas as pl
from jax.experimental.pallas import tpu as pltpu
from jax.sharding import Mesh
from jax.sharding import PartitionSpec as P

HEAD = 128
DP = ("x", "z")
COL = ("y", "k")
SIDE = 4
GROUPS = 4
PIECE_SHIFTS = (0, 3, 1, 2)
VMEM_LIMIT = 56 * 1024 * 1024
BF16 = jnp.bfloat16
F32 = jnp.float32


def shifted(value, axis, by):
    return lax.ppermute(value, axis, [(i, (i + by) % SIDE) for i in range(SIDE)])


def in_vmem():
    return pl.BlockSpec(memory_space=pltpu.VMEM)


def in_smem():
    return pl.BlockSpec(memory_space=pltpu.SMEM)


def token_blocks(tokens):
    turned = tokens.T
    half = turned.shape[0] // 2
    z = lax.axis_index("z")
    halves = turned.reshape(2, half, turned.shape[1])
    near = lax.dynamic_index_in_dim(halves, z // 2, 0, keepdims=False)
    far = lax.dynamic_index_in_dim(halves, 1 - z // 2, 0, keepdims=False)
    pairs = [(s, c) for s in range(SIDE) for c in range(2)]
    first = lax.ppermute(
        near, ("z", "k"), [(s * 2 + c, (2 * c + s // 2) * 2 + s % 2) for s, c in pairs]
    )
    second = lax.ppermute(
        far, ("z", "k"), [(s * 2 + c, (2 * c + 1 - s // 2) * 2 + s % 2) for s, c in pairs]
    )
    even = z % 2 == 0
    mine = jnp.stack([jnp.where(even, first, second), jnp.where(even, second, first)])
    filled = lax.all_gather(mine, COL, axis=0, tiled=False)
    return filled.reshape(SIDE, 2, *mine.shape)


def gathered_rows(weight):
    return shifted(weight, "x", 1), shifted(weight, "x", -1)


def turn_kernel(place, blocks, out):
    x, z = place[0], place[1]
    rows, width = blocks.shape[-2:]
    for j in range(SIDE):
        source = lax.rem(z + j, SIDE)
        pieces = [
            blocks[lax.rem(x + shift, SIDE), lax.rem(source, 2), source // 2]
            for shift in PIECE_SHIFTS
        ]
        out[width * j : width * (j + 1), :] = jnp.concatenate(pieces, axis=0).T


def turn(place, blocks):
    rows, width = blocks.shape[-2:]
    return pl.pallas_call(
        turn_kernel,
        out_shape=jax.ShapeDtypeStruct((SIDE * width, SIDE * rows), BF16),
        in_specs=[in_smem(), in_vmem()],
        out_specs=in_vmem(),
        compiler_params=pltpu.CompilerParams(vmem_limit_bytes=VMEM_LIMIT),
        cost_estimate=pl.CostEstimate(flops=0, bytes_accessed=8_000_000, transcendentals=0),
    )(place, blocks)


def project_kernel(tok, *refs):
    (q0, ql, qr, q2, k0, kl, kr, k2, out, wgt) = refs
    rows = q0.shape[0]
    width = out.shape[2]
    for part, pieces in enumerate(((q0, ql, qr, q2), (k0, kl, kr, k2))):
        for at, piece in enumerate(pieces):
            wgt[rows * at : rows * (at + 1), :] = piece[...]
        for j in range(SIDE):
            out[j, part] = jnp.dot(
                tok[width * j : width * (j + 1), :], wgt[...], preferred_element_type=F32
            ).astype(BF16)


def project(tok, pieces):
    rows, columns = pieces[0].shape
    total = tok.shape[0]
    return pl.pallas_call(
        project_kernel,
        out_shape=jax.ShapeDtypeStruct((SIDE, 2, total // SIDE, columns), BF16),
        in_specs=[in_vmem()] * 9,
        out_specs=in_vmem(),
        scratch_shapes=[pltpu.VMEM((SIDE * rows, columns), BF16)],
        compiler_params=pltpu.CompilerParams(vmem_limit_bytes=VMEM_LIMIT),
        cost_estimate=pl.CostEstimate(
            flops=2 * SIDE * rows * total * 2 * columns,
            bytes_accessed=10_000_000,
            transcendentals=0,
        ),
    )(tok, *pieces)


def attend_kernel(own, q1, q3, k1, k3, cosine, sine, allowed, out):
    heads = own.shape[2] // HEAD
    blocks = out.shape[0]
    keys = own.shape[1] // blocks
    scale = 1.0 / math.sqrt(HEAD)
    cos = cosine[...]
    sin = sine[...]
    keep = allowed[...] > 0

    def turned(part, left, right, h):
        cols = pl.ds(h * HEAD, HEAD)
        whole = (
            own[part, :, cols].astype(F32) + left[:, cols].astype(F32) + right[:, cols].astype(F32)
        )
        return (whole * cos + pltpu.roll(whole, HEAD // 2, 1) * sin).astype(BF16)

    for h in range(heads):
        query = turned(0, q1, q3, h)
        key = turned(1, k1, k3, h)
        scores = (
            lax.dot_general(key, query, (((1,), (1,)), ((), ())), preferred_element_type=F32)
            * scale
        )
        masked = jnp.where(keep, scores, -1e30)
        largest = jnp.max(masked, axis=0, keepdims=True)
        powers = jnp.exp(masked - largest)
        maps = (powers / jnp.sum(powers, axis=0, keepdims=True)).astype(BF16)
        for c in range(blocks):
            out[c, h] = maps[c * keys : (c + 1) * keys]


def attend(own, q1, q3, k1, k3, cosine, sine, allowed):
    width = own.shape[1]
    heads = own.shape[2] // HEAD
    return pl.pallas_call(
        attend_kernel,
        out_shape=jax.ShapeDtypeStruct((8, heads, width // 8, width), BF16),
        in_specs=[in_vmem()] * 8,
        out_specs=in_vmem(),
        compiler_params=pltpu.CompilerParams(vmem_limit_bytes=VMEM_LIMIT),
        cost_estimate=pl.CostEstimate(
            flops=2 * heads * HEAD * width * width,
            bytes_accessed=3_000_000,
            transcendentals=heads * width * width,
        ),
    )(own, q1, q3, k1, k3, cosine, sine, allowed)


def refine_kernel(
    owners,
    slots,
    older,
    maps,
    new_weight,
    key_ids,
    query_ids,
    pair_bias,
    gain,
    norm_bias,
    hidden_weight,
    hidden_bias,
    out_weight,
    out_bias,
    ones,
    out,
    pair,
    zeros,
    staged,
    zero_sems,
    tile_sems,
):
    step = pl.program_id(0)
    groups, per_step, queries, channels = older.shape
    count = slots.shape[0]
    tiles = owners.shape[0]
    tile = queries // tiles
    mix = pl.num_programs(0) - tiles
    keys = groups * per_step * mix

    def blank(o):
        return pltpu.make_async_copy(zeros, out.at[o], zero_sems.at[o])

    @pl.when(step == 0)
    def _():
        zeros[...] = jnp.zeros_like(zeros)
        for o in range(count):

            @pl.when(slots[o] < 0)
            def _(o=o):
                blank(o).start()

    @pl.when(step < mix)
    def _():
        fresh = lax.dot_general(
            maps[...], new_weight[...], (((0,), (0,)), ((), ())), preferred_element_type=F32
        )
        for g in range(groups):
            part = fresh[:, g * channels : (g + 1) * channels].reshape(per_step, queries, channels)
            pair[g, pl.ds(step * per_step, per_step)] = (older[g] + part + pair_bias[...]).astype(
                BF16
            )

    r = step - mix
    owner = owners[jnp.maximum(r, 0)]
    side = lax.rem(r, 2)

    def sent(owner_of, side_of):
        return pltpu.make_async_copy(
            staged.at[side_of], out.at[owner_of], tile_sems.at[side_of]
        )

    @pl.when(step >= mix + 2)
    def _():
        before = owners[r - 2]

        @pl.when(before >= 0)
        def _():
            sent(before, side).wait()

    @pl.when((step >= mix) & (owner >= 0))
    def _():
        here = pl.ds(pl.multiple_of(r * tile, tile), tile)
        wanted = query_ids[here, :]
        half = keys // 2
        low = pair[: groups // 2, :, here, :].reshape(half * tile, channels)
        high = pair[groups // 2 :, :, here, :].reshape(half * tile, channels)
        rows = jnp.concatenate([low, high], axis=1)
        values = rows.astype(F32)
        mean = jnp.dot(rows, ones[...], preferred_element_type=F32) * (1.0 / channels)
        centred = values - mean
        spread = jnp.dot(
            (centred * centred).astype(BF16), ones[...], preferred_element_type=F32
        ) * (1.0 / channels)
        normed = (centred * lax.rsqrt(spread + 1e-05) * gain[...] + norm_bias[...]).astype(BF16)
        hidden = jnp.maximum(
            jnp.dot(normed, hidden_weight[...], preferred_element_type=F32) + hidden_bias[...],
            0.0,
        ).astype(BF16)
        update = jnp.dot(hidden, out_weight[...], preferred_element_type=F32) + out_bias[...]
        result = values + update
        for part in range(2):
            piece = result[:, part * channels : (part + 1) * channels]
            piece = piece.reshape(half, tile, channels)
            same = key_ids[pl.ds(part * half, half), :][:, None, :] == wanted[None]
            staged[side, pl.ds(part * half * tile, half * tile), :] = (
                jnp.where(same, piece, 0.0).reshape(half * tile, channels).astype(BF16)
            )
        sent(owner, side).start()

    @pl.when(step == pl.num_programs(0) - 1)
    def _():
        for last in (tiles - 2, tiles - 1):

            @pl.when(owners[last] >= 0)
            def _(last=last):
                sent(owners[last], last % 2).wait()

        for o in range(count):

            @pl.when(slots[o] < 0)
            def _(o=o):
                blank(o).wait()


def refine(owners, slots, older, maps, new_weight, key_ids, query_ids, vectors):
    groups, depth, queries, channels = older.shape
    count = slots.shape[0]
    tiles = owners.shape[0]
    tile_pairs = groups * depth * queries // tiles
    mix = 4
    per_step = depth // mix
    whole = lambda a: pl.BlockSpec(a.shape, lambda i, *s, n=a.ndim: (0,) * n)
    return pl.pallas_call(
        refine_kernel,
        out_shape=jax.ShapeDtypeStruct((count, tile_pairs, channels), BF16),
        grid_spec=pltpu.PrefetchScalarGridSpec(
            num_scalar_prefetch=2,
            grid=(mix + tiles,),
            in_specs=[
                pl.BlockSpec(
                    (groups, per_step, queries, channels),
                    lambda i, *s: (0, jnp.minimum(i, mix - 1), 0, 0),
                ),
                pl.BlockSpec(
                    (maps.shape[0], per_step * queries), lambda i, *s: (0, jnp.minimum(i, mix - 1))
                ),
            ]
            + [whole(a) for a in (new_weight, key_ids, query_ids, *vectors)],
            out_specs=pl.BlockSpec(memory_space=pl.ANY),
            scratch_shapes=[
                pltpu.VMEM((groups, depth, queries, channels), BF16),
                pltpu.VMEM((tile_pairs, channels), BF16),
                pltpu.VMEM((2, tile_pairs, channels), BF16),
                pltpu.SemaphoreType.DMA((count,)),
                pltpu.SemaphoreType.DMA((2,)),
            ],
        ),
        compiler_params=pltpu.CompilerParams(vmem_limit_bytes=VMEM_LIMIT),
        cost_estimate=pl.CostEstimate(
            flops=4 * groups * depth * queries * channels * 640,
            bytes_accessed=10_000_000,
            transcendentals=0,
        ),
    )(owners, slots, older, maps, new_weight, key_ids, query_ids, *vectors)


def doubled(a, times=2):
    rows, columns = a.shape
    eye = jnp.eye(times, dtype=a.dtype)
    return (eye[:, None, :, None] * a[None, :, None, :]).reshape(times * rows, times * columns)


def chain_tokens(starts, lengths, groups, token_count):
    places = jnp.arange(token_count, dtype=jnp.int32)
    member = (places[:, None] >= starts[None, :]) & (places[:, None] < (starts + lengths)[None, :])
    inside = jnp.any(member, axis=1)
    group_ids = jnp.sum(jnp.where(member, groups[None, :], 0), axis=1)
    offset = jnp.sum(jnp.where(member, places[:, None] - starts[None, :], 0), axis=1)
    return (inside, group_ids, offset.astype(F32))


def body(
    tokens,
    query_weight,
    key_weight,
    old_maps,
    pair_weight,
    pair_bias,
    norm_gain,
    norm_bias,
    hidden_weight,
    hidden_bias,
    out_weight,
    out_bias,
    chain_starts,
    chain_lengths,
    chain_groups,
    tile_owner,
):
    row_count = lax.axis_size(DP)
    column_count = lax.axis_size(COL)
    bin_tokens = tokens.shape[0]
    block_width = bin_tokens // column_count
    place = jnp.stack([lax.axis_index("x"), lax.axis_index("z")]).astype(jnp.int32)

    blocks = token_blocks(tokens)
    q_left, q_right = gathered_rows(query_weight)
    k_left, k_right = gathered_rows(key_weight)
    q_far = shifted(q_left, "x", 1)
    k_far = shifted(k_right, "x", -1)

    inside, group_ids, offset = chain_tokens(
        chain_starts[0], chain_lengths[0], chain_groups[0], bin_tokens
    )
    ids = jnp.where(inside, group_ids, -1)
    same = (ids[:, None] == ids[None, :]) & inside[:, None]
    allowed = (same | jnp.eye(bin_tokens, dtype=bool)).astype(F32)
    half = HEAD // 2
    frequency = jnp.exp(jnp.arange(half).astype(F32) * (-2.0 * math.log(10000.0) / HEAD))
    angles = offset[:, None] * frequency[None, :]
    cosine, sine = jnp.cos(angles), jnp.sin(angles)
    cosine = jnp.concatenate([cosine, cosine], axis=1)
    sine = jnp.concatenate([-sine, sine], axis=1)
    start_key = lax.axis_index(COL) * block_width
    key_ids = jnp.where(inside, group_ids, -2).astype(F32)
    key_ids = lax.dynamic_slice_in_dim(key_ids, start_key, block_width, 0)
    key_ids = jnp.broadcast_to(key_ids[:, None], (block_width, 128))
    query_ids = jnp.broadcast_to(ids.astype(F32)[:, None], (bin_tokens, 128))
    owners = tile_owner[0, 0]
    tiles = jnp.arange(owners.shape[0], dtype=jnp.int32)
    slots = jnp.max(
        jnp.where(
            owners[None, :] == jnp.arange(row_count, dtype=jnp.int32)[:, None], tiles[None, :], -1
        ),
        axis=1,
    )

    old_channels = old_maps.shape[0]
    earlier = old_maps.reshape(old_channels, -1)
    older = jnp.dot(earlier.T, pair_weight[:old_channels], preferred_element_type=F32)
    older = older.reshape(GROUPS, block_width // GROUPS, bin_tokens, -1)
    row = lambda a: a.reshape(1, -1)
    channels = older.shape[-1]
    constants = (
        doubled(pair_weight[old_channels:], GROUPS),
        key_ids,
        query_ids,
        row(pair_bias),
        row(jnp.tile(norm_gain, 2)),
        row(jnp.tile(norm_bias, 2)),
        doubled(hidden_weight),
        row(jnp.tile(hidden_bias, 2)),
        doubled(out_weight),
        row(jnp.tile(out_bias, 2)),
        doubled(jnp.ones((channels, channels), BF16)),
    )

    blocks, older, constants, cosine, sine, allowed, slots = lax.optimization_barrier(
        (blocks, older, constants, cosine, sine, allowed, slots)
    )
    tok = turn(place, blocks)
    partial = project(
        tok, (query_weight, q_left, q_right, q_far, key_weight, k_left, k_right, k_far)
    )
    q_two = shifted(partial[2, 0], "z", 1)
    k_two = shifted(partial[2, 1], "z", -1)
    k_one = shifted(partial[1, 1], "z", 1)
    q_three = shifted(partial[3, 0], "z", -1)
    q_one = shifted(partial[1, 0] + q_two, "z", 1)
    k_three = shifted(partial[3, 1] + k_two, "z", -1)

    prob_maps = attend(partial[0], q_one, q_three, k_one, k_three, cosine, sine, allowed)
    spread_maps = lax.all_to_all(prob_maps, COL, 0, 0, tiled=True)
    heads_all = column_count * spread_maps.shape[1]
    by_group = (
        spread_maps.reshape(heads_all, GROUPS, -1).transpose(1, 0, 2).reshape(GROUPS * heads_all, -1)
    )
    outgoing = refine(
        owners, slots, older, by_group, constants[0], constants[1], constants[2], constants[3:]
    )
    arrived = lax.all_to_all(outgoing, DP, split_axis=0, concat_axis=0, tiled=True)
    return arrived.reshape(1, row_count, 1, arrived.shape[1], arrived.shape[2])


def solution(mesh):
    split = Mesh(mesh.devices.reshape(SIDE, SIDE, SIDE, 2), ("x", "z", "y", "k"))
    placed = (
        P(DP, COL),
        P(DP, COL),
        P(DP, COL),
        P(None, DP, COL, None),
        P(),
        P(),
        P(),
        P(),
        P(),
        P(),
        P(),
        P(),
        P(DP, None),
        P(DP, None),
        P(DP, None),
        P(DP, COL, None),
    )
    return jax.shard_map(
        body, mesh=split, in_specs=placed, out_specs=P(DP, None, COL, None, None), check_vma=False
    )
```

```python
import math

import jax
import jax.numpy as jnp
from jax import lax
from jax.experimental import pallas as pl
from jax.experimental.pallas import tpu as pltpu
from jax.sharding import Mesh
from jax.sharding import PartitionSpec as P

HEAD = 128
DP = ("x", "z")
COL = ("y", "k")
SIDE = 4
GROUPS = 4
PIECE_SHIFTS = (0, 3, 1, 2)
VMEM_LIMIT = 56 * 1024 * 1024
BF16 = jnp.bfloat16
F32 = jnp.float32


def shifted(value, axis, by):
    return lax.ppermute(value, axis, [(i, (i + by) % SIDE) for i in range(SIDE)])


def in_vmem():
    return pl.BlockSpec(memory_space=pltpu.VMEM)


def in_smem():
    return pl.BlockSpec(memory_space=pltpu.SMEM)


def token_blocks(tokens):
    turned = tokens.T
    half = turned.shape[0] // 2
    z = lax.axis_index("z")
    halves = turned.reshape(2, half, turned.shape[1])
    near = lax.dynamic_index_in_dim(halves, z // 2, 0, keepdims=False)
    far = lax.dynamic_index_in_dim(halves, 1 - z // 2, 0, keepdims=False)
    pairs = [(s, c) for s in range(SIDE) for c in range(2)]
    first = lax.ppermute(
        near, ("z", "k"), [(s * 2 + c, (2 * c + s // 2) * 2 + s % 2) for s, c in pairs]
    )
    second = lax.ppermute(
        far, ("z", "k"), [(s * 2 + c, (2 * c + 1 - s // 2) * 2 + s % 2) for s, c in pairs]
    )
    even = z % 2 == 0
    mine = jnp.stack([jnp.where(even, first, second), jnp.where(even, second, first)])
    filled = lax.all_gather(mine, COL, axis=0, tiled=False)
    return filled.reshape(SIDE, 2, *mine.shape)


def gathered_rows(weight):
    return shifted(weight, "x", 1), shifted(weight, "x", -1)


def turn_kernel(place, blocks, out):
    x, z = place[0], place[1]
    rows, width = blocks.shape[-2:]
    for j in range(SIDE):
        source = lax.rem(z + j, SIDE)
        pieces = [
            blocks[lax.rem(x + shift, SIDE), lax.rem(source, 2), source // 2]
            for shift in PIECE_SHIFTS
        ]
        out[width * j : width * (j + 1), :] = jnp.concatenate(pieces, axis=0).T


def turn(place, blocks):
    rows, width = blocks.shape[-2:]
    return pl.pallas_call(
        turn_kernel,
        out_shape=jax.ShapeDtypeStruct((SIDE * width, SIDE * rows), BF16),
        in_specs=[in_smem(), in_vmem()],
        out_specs=in_vmem(),
        compiler_params=pltpu.CompilerParams(vmem_limit_bytes=VMEM_LIMIT),
        cost_estimate=pl.CostEstimate(flops=0, bytes_accessed=8_000_000, transcendentals=0),
    )(place, blocks)


def project_kernel(tok, *refs):
    pieces, outs, wgt = refs[:8], refs[8:16], refs[16]
    rows, columns = pieces[0].shape
    width = outs[0].shape[0]
    for part in range(2):
        for at in range(SIDE):
            wgt[rows * at : rows * (at + 1), columns * part : columns * (part + 1)] = pieces[
                SIDE * part + at
            ][...]
    whole = jnp.dot(tok[...], wgt[...], preferred_element_type=F32).astype(BF16)
    for j in range(SIDE):
        for part in range(2):
            outs[2 * j + part][...] = whole[
                width * j : width * (j + 1), columns * part : columns * (part + 1)
            ]


def project(tok, pieces):
    rows, columns = pieces[0].shape
    total = tok.shape[0]
    return pl.pallas_call(
        project_kernel,
        out_shape=[jax.ShapeDtypeStruct((total // SIDE, columns), BF16)] * 8,
        in_specs=[in_vmem()] * 9,
        out_specs=[in_vmem()] * 8,
        scratch_shapes=[pltpu.VMEM((SIDE * rows, 2 * columns), BF16)],
        compiler_params=pltpu.CompilerParams(vmem_limit_bytes=VMEM_LIMIT),
        cost_estimate=pl.CostEstimate(
            flops=2 * SIDE * rows * total * 2 * columns,
            bytes_accessed=10_000_000,
            transcendentals=0,
        ),
    )(tok, *pieces)


def add_kernel(a, b, c, d, first, second):
    first[...] = (a[...].astype(F32) + b[...].astype(F32)).astype(BF16)
    second[...] = (c[...].astype(F32) + d[...].astype(F32)).astype(BF16)


def two_sums(a, b, c, d):
    shape = jax.ShapeDtypeStruct(a.shape, a.dtype)
    return pl.pallas_call(
        add_kernel,
        out_shape=[shape] * 2,
        in_specs=[in_vmem()] * 4,
        out_specs=[in_vmem()] * 2,
        cost_estimate=pl.CostEstimate(flops=a.size * 2, bytes_accessed=2_000_000, transcendentals=0),
    )(a, b, c, d)


def attend_kernel(place, q0, q1, q3, k0, k1, k3, cosine, sine, allowed, *outs):
    *outs, held = outs
    heads = q0.shape[1] // HEAD
    cores, sides = outs[0].shape[0], len(outs)
    keys = q0.shape[0] // (cores * sides)
    scale = 1.0 / math.sqrt(HEAD)
    cos = cosine[...]
    sin = sine[...]
    keep = allowed[...] > 0

    def turned(parts, h):
        cols = pl.ds(h * HEAD, HEAD)
        own, left, right = parts
        whole = own[:, cols].astype(F32) + left[:, cols].astype(F32) + right[:, cols].astype(F32)
        return (whole * cos + pltpu.roll(whole, HEAD // 2, 1) * sin).astype(BF16)

    for h in range(heads):
        query = turned((q0, q1, q3), h)
        key = turned((k0, k1, k3), h)
        scores = (
            lax.dot_general(key, query, (((1,), (1,)), ((), ())), preferred_element_type=F32)
            * scale
        )
        masked = jnp.where(keep, scores, -1e30)
        largest = jnp.max(masked, axis=0, keepdims=True)
        powers = jnp.exp(masked - largest)
        held[...] = (powers / jnp.sum(powers, axis=0, keepdims=True)).astype(BF16)
        for side, out in enumerate(outs):
            for core in range(cores):
                block = lax.rem(place[2] + side, sides) * cores + lax.rem(place[3] + core, cores)
                mine = pl.ds(pl.multiple_of(block * keys, keys), keys)
                out[core, h] = held[mine, :]


def attend(place, *operands):
    width, columns = operands[0].shape
    heads = columns // HEAD
    return pl.pallas_call(
        attend_kernel,
        out_shape=[jax.ShapeDtypeStruct((2, heads, width // 8, width), BF16)] * SIDE,
        in_specs=[in_smem()] + [in_vmem()] * 9,
        out_specs=[in_vmem()] * SIDE,
        scratch_shapes=[pltpu.VMEM((width, width), BF16)],
        compiler_params=pltpu.CompilerParams(vmem_limit_bytes=VMEM_LIMIT),
        cost_estimate=pl.CostEstimate(
            flops=2 * heads * HEAD * width * width,
            bytes_accessed=3_000_000,
            transcendentals=heads * width * width,
        ),
    )(place, *operands)


def refine_kernel(
    owners,
    older,
    maps,
    new_weight,
    key_ids,
    query_ids,
    pair_bias,
    gain,
    norm_bias,
    hidden_weight,
    hidden_bias,
    out_weight,
    out_bias,
    ones,
    out,
    zeros,
    staged,
    zero_sems,
    tile_sems,
):
    step = pl.program_id(0)
    keys, queries, channels = older.shape
    count = out.shape[0]
    tiles = owners.shape[0]
    tile = queries // tiles
    each = keys // GROUPS
    rows = each * queries

    def empty(o):
        none = owners[0] != o
        for i in range(1, tiles):
            none = none & (owners[i] != o)
        return none

    def blank(o):
        return pltpu.make_async_copy(zeros, out.at[o], zero_sems.at[o])

    def sent(r):
        some = pl.ds(pl.multiple_of(step * keys * tile, keys * tile), keys * tile)
        return pltpu.make_async_copy(
            staged.at[r, some], out.at[owners[r], some], tile_sems.at[step, r]
        )

    @pl.when(step == 0)
    def _():
        zeros[...] = jnp.zeros_like(zeros)
        for o in range(count):

            @pl.when(empty(o))
            def _(o=o):
                blank(o).start()

    fresh = lax.dot_general(
        maps[...], new_weight[...], (((0,), (0,)), ((), ())), preferred_element_type=F32
    )
    for couple in range(GROUPS // 2):
        groups = (2 * couple, 2 * couple + 1)
        pair = jnp.concatenate(
            [
                older[each * g : each * (g + 1)].reshape(rows, channels)
                + fresh[:, g * channels : (g + 1) * channels]
                + pair_bias[...]
                for g in groups
            ],
            axis=1,
        ).astype(BF16)
        values = pair.astype(F32)
        mean = jnp.dot(pair, ones[...], preferred_element_type=F32) * (1.0 / channels)
        centred = values - mean
        spread = jnp.dot(
            (centred * centred).astype(BF16), ones[...], preferred_element_type=F32
        ) * (1.0 / channels)
        normed = (centred * lax.rsqrt(spread + 1e-05) * gain[...] + norm_bias[...]).astype(BF16)
        hidden = jnp.maximum(
            jnp.dot(normed, hidden_weight[...], preferred_element_type=F32) + hidden_bias[...],
            0.0,
        ).astype(BF16)
        update = jnp.dot(hidden, out_weight[...], preferred_element_type=F32) + out_bias[...]
        result = values + update
        for side, g in enumerate(groups):
            for e in range(each):
                u = step * keys + each * g + e
                piece = result[
                    e * queries : (e + 1) * queries, side * channels : (side + 1) * channels
                ]
                same = key_ids[pl.ds(u, 1), :] == query_ids[...]
                piece = jnp.where(same, piece, 0.0).astype(BF16)
                at = pl.ds(pl.multiple_of(u * tile, tile), tile)
                for r in range(tiles):
                    staged[r, at, :] = piece[r * tile : (r + 1) * tile]

    for r in range(tiles):

        @pl.when(owners[r] >= 0)
        def _(r=r):
            sent(r).start()

    @pl.when(step == pl.num_programs(0) - 1)
    def _():
        for r in range(tiles):

            @pl.when(owners[r] >= 0)
            def _(r=r):
                for s in range(SIDE):
                    some = pl.ds(s * keys * tile, keys * tile)
                    pltpu.make_async_copy(
                        staged.at[r, some], out.at[owners[r], some], tile_sems.at[s, r]
                    ).wait()

        for o in range(count):

            @pl.when(empty(o))
            def _(o=o):
                blank(o).wait()


def refine(owners, count, older, maps, new_weight, key_ids, query_ids, vectors):
    keys, queries, channels = older.shape
    tiles = owners.shape[0]
    tile_pairs = keys * queries // tiles
    whole = lambda a: pl.BlockSpec(a.shape, lambda i, *s, n=a.ndim: (0,) * n)
    return pl.pallas_call(
        refine_kernel,
        out_shape=jax.ShapeDtypeStruct((count, tile_pairs, channels), BF16),
        grid_spec=pltpu.PrefetchScalarGridSpec(
            num_scalar_prefetch=1,
            grid=(SIDE,),
            in_specs=[
                pl.BlockSpec((keys // SIDE, queries, channels), lambda i, *s: (i, 0, 0)),
                pl.BlockSpec((maps.shape[0], maps.shape[1] // SIDE), lambda i, *s: (0, i)),
            ]
            + [whole(a) for a in (new_weight, key_ids, query_ids, *vectors)],
            out_specs=pl.BlockSpec(memory_space=pl.ANY),
            scratch_shapes=[
                pltpu.VMEM((tile_pairs, channels), BF16),
                pltpu.VMEM((tiles, tile_pairs, channels), BF16),
                pltpu.SemaphoreType.DMA((count,)),
                pltpu.SemaphoreType.DMA((SIDE, tiles)),
            ],
        ),
        compiler_params=pltpu.CompilerParams(vmem_limit_bytes=VMEM_LIMIT),
        cost_estimate=pl.CostEstimate(
            flops=4 * keys * queries * channels * 640,
            bytes_accessed=10_000_000,
            transcendentals=0,
        ),
    )(owners, older, maps, new_weight, key_ids, query_ids, *vectors)


def prepare_kernel(
    place,
    starts,
    lengths,
    groups,
    pair_weight,
    gain,
    norm_bias,
    hidden_weight,
    hidden_bias,
    out_weight,
    out_bias,
    new_out,
    key_out,
    query_out,
    gain_out,
    norm_out,
    hidden_out,
    hbias_out,
    weight_out,
    obias_out,
    ones_out,
    cos_out,
    sin_out,
    allowed_out,
):
    channels = gain.shape[1]
    hidden = hidden_bias.shape[1]
    tokens = allowed_out.shape[0]
    keys = key_out.shape[0]
    chains = starts.shape[1]

    def described(places, outside):
        ids = jnp.full(places.shape, outside, jnp.int32)
        offset = jnp.zeros(places.shape, jnp.int32)
        for c in range(chains):
            first = starts[0, c]
            member = (places >= first) & (places < first + lengths[0, c])
            ids = jnp.where(member, groups[0, c], ids)
            offset = jnp.where(member, places - first, offset)
        return ids, offset

    iota = lambda shape, dim: lax.broadcasted_iota(jnp.int32, shape, dim)
    by_row, offset = described(iota((tokens, HEAD), 0), -1)
    query_out[...] = by_row.astype(F32)
    first_key = (place[2] * 2 + place[3]) * keys
    key_out[...] = described(iota((keys, HEAD), 0) + first_key, -2)[0].astype(F32)
    square = (tokens, tokens)
    rows, columns = iota(square, 0), iota(square, 1)
    same = described(rows, -1)[0] == described(columns, -2)[0]
    allowed_out[...] = jnp.where(same | (rows == columns), 1.0, 0.0)

    half = HEAD // 2
    lane = iota((tokens, HEAD), 1)
    frequency = jnp.exp(
        lax.rem(lane, half).astype(F32) * (-2.0 * math.log(10000.0) / HEAD)
    )
    angles = offset.astype(F32) * frequency
    cos_out[...] = jnp.cos(angles)
    sine = jnp.sin(angles)
    sin_out[...] = jnp.where(lane < half, -sine, sine)

    for ref, out in ((gain, gain_out), (norm_bias, norm_out), (out_bias, obias_out)):
        out[:, :channels] = ref[...]
        out[:, channels:] = ref[...]
    hbias_out[:, :hidden] = hidden_bias[...]
    hbias_out[:, hidden:] = hidden_bias[...]
    hidden_out[...] = jnp.zeros_like(hidden_out)
    hidden_out[:channels, :hidden] = hidden_weight[...]
    hidden_out[channels:, hidden:] = hidden_weight[...]
    weight_out[...] = jnp.zeros_like(weight_out)
    weight_out[:hidden, :channels] = out_weight[...]
    weight_out[hidden:, channels:] = out_weight[...]
    shape = ones_out.shape
    ones_out[...] = jnp.where(
        iota(shape, 0) // channels == iota(shape, 1) // channels, 1.0, 0.0
    ).astype(BF16)

    heads_all = new_out.shape[0] // GROUPS
    per_side = heads_all // SIDE
    shape = (new_out.shape[0], heads_all)
    row = iota(shape, 0) // GROUPS
    per_core = per_side // 2
    piece = lax.rem(row // per_core, SIDE)
    shift = jnp.where(piece == 1, 3, jnp.where(piece == 2, 1, jnp.where(piece == 3, 2, 0)))
    core = lax.rem(row // (per_core * SIDE) + place[3], 2)
    head = lax.rem(place[2] + shift, SIDE) * per_side + core * per_core + lax.rem(row, per_core)
    chosen = jnp.where(iota(shape, 1) == head, 1.0, 0.0).astype(BF16)
    old = pair_weight.shape[0] - heads_all
    repeated = jnp.dot(chosen, pair_weight[old:, :], preferred_element_type=F32)
    group = lax.rem(iota(repeated.shape, 0), GROUPS)
    for g in range(GROUPS):
        new_out[:, g * channels : (g + 1) * channels] = jnp.where(
            group == g, repeated, 0.0
        ).astype(BF16)


def prepare(place, chains, pair_weight, vectors, tokens):
    gain, hidden_bias = vectors[0], vectors[3]
    channels, hidden = gain.shape[1], hidden_bias.shape[1]
    heads_all = tokens.shape[1] * 8 // HEAD
    count = tokens.shape[0]
    new_shape = (heads_all * GROUPS, GROUPS * channels)
    shapes = [
        (new_shape, BF16),
        ((count // 8, channels), F32),
        ((count, channels), F32),
        ((1, 2 * channels), F32),
        ((1, 2 * channels), F32),
        ((2 * channels, 2 * hidden), BF16),
        ((1, 2 * hidden), F32),
        ((2 * hidden, 2 * channels), BF16),
        ((1, 2 * channels), F32),
        ((2 * channels, 2 * channels), BF16),
        ((count, HEAD), F32),
        ((count, HEAD), F32),
        ((count, count), F32),
    ]
    return pl.pallas_call(
        prepare_kernel,
        out_shape=[jax.ShapeDtypeStruct(*s) for s in shapes],
        in_specs=[in_smem()] * 4 + [in_vmem()] * 7,
        out_specs=[in_vmem()] * len(shapes),
        compiler_params=pltpu.CompilerParams(vmem_limit_bytes=VMEM_LIMIT),
        cost_estimate=pl.CostEstimate(
            flops=10_000_000, bytes_accessed=4_000_000, transcendentals=100_000
        ),
    )(place, *chains, pair_weight, *vectors)


def body(
    tokens,
    query_weight,
    key_weight,
    old_maps,
    pair_weight,
    pair_bias,
    norm_gain,
    norm_bias,
    hidden_weight,
    hidden_bias,
    out_weight,
    out_bias,
    chain_starts,
    chain_lengths,
    chain_groups,
    tile_owner,
):
    row_count = lax.axis_size(DP)
    column_count = lax.axis_size(COL)
    bin_tokens = tokens.shape[0]
    block_width = bin_tokens // column_count
    place = jnp.stack([lax.axis_index(a) for a in ("x", "z", "y", "k")])
    place = place.astype(jnp.int32)

    q_left, q_right = gathered_rows(query_weight)
    k_left, k_right = gathered_rows(key_weight)
    old_channels = old_maps.shape[0]
    earlier = old_maps.reshape(old_channels, -1)
    q_left, k_right, earlier = lax.optimization_barrier((q_left, k_right, earlier))
    q_far = shifted(q_left, "x", 1)
    k_far = shifted(k_right, "x", -1)
    blocks = token_blocks(tokens)
    tok = turn(place, blocks)
    partial = project(
        tok, (query_weight, q_left, q_right, q_far, key_weight, k_left, k_right, k_far)
    )
    partial, earlier, chains = lax.optimization_barrier(
        (partial, earlier, (chain_starts, chain_lengths, chain_groups))
    )
    row = lambda a: a.reshape(1, -1)
    prepared = prepare(
        place,
        chains,
        pair_weight,
        (
            row(norm_gain),
            row(norm_bias),
            hidden_weight,
            row(hidden_bias),
            out_weight,
            row(out_bias),
        ),
        tokens,
    )
    older = jnp.dot(earlier.T, pair_weight[:old_channels], preferred_element_type=F32)
    older = older.reshape(block_width, bin_tokens, -1)
    q_zero, k_zero, q_one, k_one, q_three, k_three, q_two, k_two = (
        partial[i] for i in (0, 1, 2, 3, 6, 7, 4, 5)
    )
    q_two = shifted(q_two, "z", 1)
    k_two = shifted(k_two, "z", -1)
    k_one = shifted(k_one, "z", 1)
    q_three = shifted(q_three, "z", -1)
    q_two, k_two, prepared = lax.optimization_barrier((q_two, k_two, prepared))
    new_weight, key_ids, query_ids = prepared[:3]
    vectors = (row(pair_bias), *prepared[3:10])
    cosine, sine, allowed = prepared[10:]
    q_one, k_three = two_sums(q_one, q_two, k_three, k_two)
    q_one = shifted(q_one, "z", 1)
    k_three = shifted(k_three, "z", -1)
    q_one, k_three, older = lax.optimization_barrier((q_one, k_three, older))

    maps = attend(
        place, q_zero, q_one, q_three, k_zero, k_one, k_three, cosine, sine, allowed
    )
    pieces = [maps[0]] + [shifted(maps[s % SIDE], "y", s) for s in (1, -1, 2)]
    other = lax.ppermute(jnp.stack([p[1] for p in pieces]), "k", [(0, 1), (1, 0)])
    spread_maps = jnp.concatenate([jnp.stack([p[0] for p in pieces]), other])
    by_group = spread_maps.reshape(-1, SIDE, GROUPS, 2, bin_tokens).transpose(0, 2, 1, 3, 4)
    by_group = by_group.reshape(-1, SIDE * 2 * bin_tokens)
    outgoing = refine(
        tile_owner[0, 0], row_count, older, by_group, new_weight, key_ids, query_ids, vectors
    )
    arrived = lax.all_to_all(outgoing, DP, split_axis=0, concat_axis=0, tiled=True)
    return arrived.reshape(1, row_count, 1, arrived.shape[1], arrived.shape[2])


def solution(mesh):
    split = Mesh(mesh.devices.reshape(SIDE, SIDE, SIDE, 2), ("x", "z", "y", "k"))
    placed = (
        P(DP, COL),
        P(DP, COL),
        P(DP, COL),
        P(None, DP, COL, None),
        P(),
        P(),
        P(),
        P(),
        P(),
        P(),
        P(),
        P(),
        P(DP, None),
        P(DP, None),
        P(DP, None),
        P(DP, COL, None),
    )
    return jax.shard_map(
        body, mesh=split, in_specs=placed, out_specs=P(DP, None, COL, None, None), check_vma=False
    )
```

```python
import math

import jax
import jax.numpy as jnp
from jax import lax
from jax.experimental import pallas as pl
from jax.experimental.pallas import tpu as pltpu
from jax.sharding import Mesh
from jax.sharding import PartitionSpec as P

HEAD = 128
DP = ("x", "z")
COL = ("y", "k")
SIDE = 4
GROUPS = 4
PIECE_SHIFTS = (0, 3, 1, 2)
VMEM_LIMIT = 28 * 1024 * 1024
BF16 = jnp.bfloat16
F32 = jnp.float32


def shifted(value, axis, by):
    return lax.ppermute(value, axis, [(i, (i + by) % SIDE) for i in range(SIDE)])


def in_vmem():
    return pl.BlockSpec(memory_space=pltpu.VMEM)


def in_smem():
    return pl.BlockSpec(memory_space=pltpu.SMEM)


def token_blocks(tokens):
    turned = tokens.T
    half = turned.shape[0] // 2
    z = lax.axis_index("z")
    halves = turned.reshape(2, half, turned.shape[1])
    near = lax.dynamic_index_in_dim(halves, z // 2, 0, keepdims=False)
    far = lax.dynamic_index_in_dim(halves, 1 - z // 2, 0, keepdims=False)
    pairs = [(s, c) for s in range(SIDE) for c in range(2)]
    first = lax.ppermute(
        near, ("z", "k"), [(s * 2 + c, (2 * c + s // 2) * 2 + s % 2) for s, c in pairs]
    )
    second = lax.ppermute(
        far, ("z", "k"), [(s * 2 + c, (2 * c + 1 - s // 2) * 2 + s % 2) for s, c in pairs]
    )
    even = z % 2 == 0
    mine = jnp.stack([jnp.where(even, first, second), jnp.where(even, second, first)])
    filled = lax.all_gather(mine, COL, axis=0, tiled=False)
    return filled.reshape(SIDE, 2, *mine.shape)


def gathered_rows(weight):
    return shifted(weight, "x", 1), shifted(weight, "x", -1)


def turn_kernel(place, blocks, out):
    x, z = place[0], place[1]
    rows, width = blocks.shape[-2:]
    for j in range(SIDE):
        source = lax.rem(z + j, SIDE)
        pieces = [
            blocks[lax.rem(x + shift, SIDE), lax.rem(source, 2), source // 2]
            for shift in PIECE_SHIFTS
        ]
        out[width * j : width * (j + 1), :] = jnp.concatenate(pieces, axis=0).T


def turn(place, blocks):
    rows, width = blocks.shape[-2:]
    return pl.pallas_call(
        turn_kernel,
        out_shape=jax.ShapeDtypeStruct((SIDE * width, SIDE * rows), BF16),
        in_specs=[in_smem(), in_vmem()],
        out_specs=in_vmem(),
        compiler_params=pltpu.CompilerParams(vmem_limit_bytes=VMEM_LIMIT),
        cost_estimate=pl.CostEstimate(flops=0, bytes_accessed=8_000_000, transcendentals=0),
    )(place, blocks)


def project_kernel(tok, *refs):
    pieces, outs, wgt = refs[:8], refs[8:16], refs[16]
    rows, columns = pieces[0].shape
    width = outs[0].shape[0]
    for part in range(2):
        for at in range(SIDE):
            wgt[rows * at : rows * (at + 1), columns * part : columns * (part + 1)] = pieces[
                SIDE * part + at
            ][...]
    whole = jnp.dot(tok[...], wgt[...], preferred_element_type=F32).astype(BF16)
    for j in range(SIDE):
        for part in range(2):
            outs[2 * j + part][...] = whole[
                width * j : width * (j + 1), columns * part : columns * (part + 1)
            ]


def project(tok, pieces):
    rows, columns = pieces[0].shape
    total = tok.shape[0]
    return pl.pallas_call(
        project_kernel,
        out_shape=[jax.ShapeDtypeStruct((total // SIDE, columns), BF16)] * 8,
        in_specs=[in_vmem()] * 9,
        out_specs=[in_vmem()] * 8,
        scratch_shapes=[pltpu.VMEM((SIDE * rows, 2 * columns), BF16)],
        compiler_params=pltpu.CompilerParams(vmem_limit_bytes=VMEM_LIMIT),
        cost_estimate=pl.CostEstimate(
            flops=2 * SIDE * rows * total * 2 * columns,
            bytes_accessed=10_000_000,
            transcendentals=0,
        ),
    )(tok, *pieces)


def add_kernel(a, b, c, d, first, second):
    first[...] = (a[...].astype(F32) + b[...].astype(F32)).astype(BF16)
    second[...] = (c[...].astype(F32) + d[...].astype(F32)).astype(BF16)


def two_sums(a, b, c, d):
    shape = jax.ShapeDtypeStruct(a.shape, a.dtype)
    return pl.pallas_call(
        add_kernel,
        out_shape=[shape] * 2,
        in_specs=[in_vmem()] * 4,
        out_specs=[in_vmem()] * 2,
        cost_estimate=pl.CostEstimate(flops=a.size * 2, bytes_accessed=2_000_000, transcendentals=0),
    )(a, b, c, d)


def attend_kernel(place, q0, q1, q3, k0, k1, k3, cosine, sine, allowed, *outs):
    *outs, held = outs
    heads = q0.shape[1] // HEAD
    cores, sides = 2, len(outs) // 2
    keys = q0.shape[0] // (cores * sides)
    scale = 1.0 / math.sqrt(HEAD)
    cos = cosine[...]
    sin = sine[...]
    keep = allowed[...] > 0

    def turned(parts, h):
        cols = pl.ds(h * HEAD, HEAD)
        own, left, right = parts
        whole = own[:, cols].astype(F32) + left[:, cols].astype(F32) + right[:, cols].astype(F32)
        return (whole * cos + pltpu.roll(whole, HEAD // 2, 1) * sin).astype(BF16)

    for h in range(heads):
        query = turned((q0, q1, q3), h)
        key = turned((k0, k1, k3), h)
        scores = (
            lax.dot_general(key, query, (((1,), (1,)), ((), ())), preferred_element_type=F32)
            * scale
        )
        masked = jnp.where(keep, scores, -1e30)
        largest = jnp.max(masked, axis=0, keepdims=True)
        powers = jnp.exp(masked - largest)
        held[...] = (powers / jnp.sum(powers, axis=0, keepdims=True)).astype(BF16)
        for side in range(sides):
            for core in range(cores):
                block = lax.rem(place[2] + side, sides) * cores + lax.rem(place[3] + core, cores)
                mine = pl.ds(pl.multiple_of(block * keys, keys), keys)
                outs[core * sides + side][h] = held[mine, :]


def attend(place, *operands):
    width, columns = operands[0].shape
    heads = columns // HEAD
    return pl.pallas_call(
        attend_kernel,
        out_shape=[jax.ShapeDtypeStruct((heads, width // 8, width), BF16)] * (2 * SIDE),
        in_specs=[in_smem()] + [in_vmem()] * 9,
        out_specs=[in_vmem()] * (2 * SIDE),
        scratch_shapes=[pltpu.VMEM((width, width), BF16)],
        compiler_params=pltpu.CompilerParams(vmem_limit_bytes=VMEM_LIMIT),
        cost_estimate=pl.CostEstimate(
            flops=2 * heads * HEAD * width * width,
            bytes_accessed=3_000_000,
            transcendentals=heads * width * width,
        ),
    )(place, *operands)


def older_kernel(maps, weight, *refs):
    out = refs[-1]
    turned = weight[: maps.shape[0], :].T
    by_key = jnp.swapaxes(maps[:, 0], 0, 1)
    for u in range(maps.shape[2]):
        out[u] = jnp.dot(turned, by_key[u], preferred_element_type=F32).T


def older_part(half, maps, weight, before=None):
    depth, _, keys, queries = maps.shape
    channels = weight.shape[1]
    some = keys // 2
    extra = () if before is None else (before,)
    return pl.pallas_call(
        older_kernel,
        out_shape=jax.ShapeDtypeStruct((keys, queries, channels), F32),
        grid=(1,),
        in_specs=[
            pl.BlockSpec((depth, 1, some, queries), lambda i: (0, 0, half, 0)),
            pl.BlockSpec(weight.shape, lambda i: (0, 0)),
        ]
        + [pl.BlockSpec(memory_space=pl.ANY)] * len(extra),
        out_specs=pl.BlockSpec((some, queries, channels), lambda i: (half, 0, 0)),
        input_output_aliases={2: 0} if extra else {},
        compiler_params=pltpu.CompilerParams(vmem_limit_bytes=40 * 1024 * 1024),
        cost_estimate=pl.CostEstimate(
            flops=2 * depth * some * queries * channels,
            bytes_accessed=2 * depth * some * queries,
            transcendentals=0,
        ),
    )(maps, weight, *extra)


def refine_kernel(
    owners,
    older,
    maps,
    new_weight,
    key_ids,
    query_ids,
    pair_bias,
    gain,
    norm_bias,
    hidden_weight,
    hidden_bias,
    out_weight,
    out_bias,
    ones,
    out,
    zeros,
    staged,
    zero_sems,
    tile_sems,
):
    step = pl.program_id(0)
    keys, queries, channels = older.shape
    count = out.shape[0]
    tiles = owners.shape[0]
    tile = queries // tiles
    each = keys // GROUPS
    rows = each * queries

    def empty(o):
        none = owners[0] != o
        for i in range(1, tiles):
            none = none & (owners[i] != o)
        return none

    def blank(o):
        return pltpu.make_async_copy(zeros, out.at[o], zero_sems.at[o])

    def sent(r):
        some = pl.ds(pl.multiple_of(step * keys * tile, keys * tile), keys * tile)
        return pltpu.make_async_copy(
            staged.at[r, some], out.at[owners[r], some], tile_sems.at[step, r]
        )

    @pl.when(step == 0)
    def _():
        zeros[...] = jnp.zeros_like(zeros)
        for o in range(count):

            @pl.when(empty(o))
            def _(o=o):
                blank(o).start()

    fresh = lax.dot_general(
        maps[...], new_weight[...], (((0,), (0,)), ((), ())), preferred_element_type=F32
    )
    for couple in range(GROUPS // 2):
        groups = (2 * couple, 2 * couple + 1)
        pair = jnp.concatenate(
            [
                older[each * g : each * (g + 1)].reshape(rows, channels)
                + fresh[:, g * channels : (g + 1) * channels]
                + pair_bias[...]
                for g in groups
            ],
            axis=1,
        ).astype(BF16)
        values = pair.astype(F32)
        mean = jnp.dot(pair, ones[...], preferred_element_type=F32) * (1.0 / channels)
        centred = values - mean
        spread = jnp.dot(
            (centred * centred).astype(BF16), ones[...], preferred_element_type=F32
        ) * (1.0 / channels)
        normed = (centred * lax.rsqrt(spread + 1e-05) * gain[...] + norm_bias[...]).astype(BF16)
        hidden = jnp.maximum(
            jnp.dot(normed, hidden_weight[...], preferred_element_type=F32) + hidden_bias[...],
            0.0,
        ).astype(BF16)
        update = jnp.dot(hidden, out_weight[...], preferred_element_type=F32) + out_bias[...]
        result = values + update
        for side, g in enumerate(groups):
            for e in range(each):
                u = step * keys + each * g + e
                piece = result[
                    e * queries : (e + 1) * queries, side * channels : (side + 1) * channels
                ]
                same = key_ids[pl.ds(u, 1), :] == query_ids[...]
                piece = jnp.where(same, piece, 0.0).astype(BF16)
                at = pl.ds(pl.multiple_of(u * tile, tile), tile)
                for r in range(tiles):
                    staged[r, at, :] = piece[r * tile : (r + 1) * tile]

    for r in range(tiles):

        @pl.when(owners[r] >= 0)
        def _(r=r):
            sent(r).start()

    @pl.when(step == pl.num_programs(0) - 1)
    def _():
        for r in range(tiles):

            @pl.when(owners[r] >= 0)
            def _(r=r):
                for s in range(SIDE):
                    some = pl.ds(s * keys * tile, keys * tile)
                    pltpu.make_async_copy(
                        staged.at[r, some], out.at[owners[r], some], tile_sems.at[s, r]
                    ).wait()

        for o in range(count):

            @pl.when(empty(o))
            def _(o=o):
                blank(o).wait()


def refine(owners, count, older, maps, new_weight, key_ids, query_ids, vectors):
    keys, queries, channels = older.shape
    tiles = owners.shape[0]
    tile_pairs = keys * queries // tiles
    whole = lambda a: pl.BlockSpec(a.shape, lambda i, *s, n=a.ndim: (0,) * n)
    return pl.pallas_call(
        refine_kernel,
        out_shape=jax.ShapeDtypeStruct((count, tile_pairs, channels), BF16),
        grid_spec=pltpu.PrefetchScalarGridSpec(
            num_scalar_prefetch=1,
            grid=(SIDE,),
            in_specs=[
                pl.BlockSpec((keys // SIDE, queries, channels), lambda i, *s: (i, 0, 0)),
                pl.BlockSpec((maps.shape[0], maps.shape[1] // SIDE), lambda i, *s: (0, i)),
            ]
            + [whole(a) for a in (new_weight, key_ids, query_ids, *vectors)],
            out_specs=pl.BlockSpec(memory_space=pl.ANY),
            scratch_shapes=[
                pltpu.VMEM((tile_pairs, channels), BF16),
                pltpu.VMEM((tiles, tile_pairs, channels), BF16),
                pltpu.SemaphoreType.DMA((count,)),
                pltpu.SemaphoreType.DMA((SIDE, tiles)),
            ],
        ),
        compiler_params=pltpu.CompilerParams(vmem_limit_bytes=VMEM_LIMIT),
        cost_estimate=pl.CostEstimate(
            flops=4 * keys * queries * channels * 640,
            bytes_accessed=10_000_000,
            transcendentals=0,
        ),
    )(owners, older, maps, new_weight, key_ids, query_ids, *vectors)


def prepare_kernel(
    place,
    starts,
    lengths,
    groups,
    pair_weight,
    gain,
    norm_bias,
    hidden_weight,
    hidden_bias,
    out_weight,
    out_bias,
    new_out,
    key_out,
    query_out,
    gain_out,
    norm_out,
    hidden_out,
    hbias_out,
    weight_out,
    obias_out,
    ones_out,
    cos_out,
    sin_out,
    allowed_out,
):
    channels = gain.shape[1]
    hidden = hidden_bias.shape[1]
    tokens = allowed_out.shape[0]
    keys = key_out.shape[0]
    chains = starts.shape[1]

    def described(places, outside):
        ids = jnp.full(places.shape, outside, jnp.int32)
        offset = jnp.zeros(places.shape, jnp.int32)
        for c in range(chains):
            first = starts[0, c]
            member = (places >= first) & (places < first + lengths[0, c])
            ids = jnp.where(member, groups[0, c], ids)
            offset = jnp.where(member, places - first, offset)
        return ids, offset

    iota = lambda shape, dim: lax.broadcasted_iota(jnp.int32, shape, dim)
    by_row, offset = described(iota((tokens, HEAD), 0), -1)
    query_out[...] = by_row.astype(F32)
    first_key = (place[2] * 2 + place[3]) * keys
    key_out[...] = described(iota((keys, HEAD), 0) + first_key, -2)[0].astype(F32)
    square = (tokens, tokens)
    rows, columns = iota(square, 0), iota(square, 1)
    same = described(rows, -1)[0] == described(columns, -2)[0]
    allowed_out[...] = jnp.where(same | (rows == columns), 1.0, 0.0)

    half = HEAD // 2
    lane = iota((tokens, HEAD), 1)
    frequency = jnp.exp(
        lax.rem(lane, half).astype(F32) * (-2.0 * math.log(10000.0) / HEAD)
    )
    angles = offset.astype(F32) * frequency
    cos_out[...] = jnp.cos(angles)
    sine = jnp.sin(angles)
    sin_out[...] = jnp.where(lane < half, -sine, sine)

    for ref, out in ((gain, gain_out), (norm_bias, norm_out), (out_bias, obias_out)):
        out[:, :channels] = ref[...]
        out[:, channels:] = ref[...]
    hbias_out[:, :hidden] = hidden_bias[...]
    hbias_out[:, hidden:] = hidden_bias[...]
    hidden_out[...] = jnp.zeros_like(hidden_out)
    hidden_out[:channels, :hidden] = hidden_weight[...]
    hidden_out[channels:, hidden:] = hidden_weight[...]
    weight_out[...] = jnp.zeros_like(weight_out)
    weight_out[:hidden, :channels] = out_weight[...]
    weight_out[hidden:, channels:] = out_weight[...]
    shape = ones_out.shape
    ones_out[...] = jnp.where(
        iota(shape, 0) // channels == iota(shape, 1) // channels, 1.0, 0.0
    ).astype(BF16)

    heads_all = new_out.shape[0] // GROUPS
    per_side = heads_all // SIDE
    shape = (new_out.shape[0], heads_all)
    row = iota(shape, 0) // GROUPS
    per_core = per_side // 2
    piece = lax.rem(row // per_core, SIDE)
    shift = jnp.where(piece == 1, 3, jnp.where(piece == 2, 1, jnp.where(piece == 3, 2, 0)))
    core = lax.rem(row // (per_core * SIDE) + place[3], 2)
    head = lax.rem(place[2] + shift, SIDE) * per_side + core * per_core + lax.rem(row, per_core)
    chosen = jnp.where(iota(shape, 1) == head, 1.0, 0.0).astype(BF16)
    old = pair_weight.shape[0] - heads_all
    repeated = jnp.dot(chosen, pair_weight[old:, :], preferred_element_type=F32)
    group = lax.rem(iota(repeated.shape, 0), GROUPS)
    for g in range(GROUPS):
        new_out[:, g * channels : (g + 1) * channels] = jnp.where(
            group == g, repeated, 0.0
        ).astype(BF16)


def prepare(place, chains, pair_weight, vectors, tokens):
    gain, hidden_bias = vectors[0], vectors[3]
    channels, hidden = gain.shape[1], hidden_bias.shape[1]
    heads_all = tokens.shape[1] * 8 // HEAD
    count = tokens.shape[0]
    new_shape = (heads_all * GROUPS, GROUPS * channels)
    shapes = [
        (new_shape, BF16),
        ((count // 8, channels), F32),
        ((count, channels), F32),
        ((1, 2 * channels), F32),
        ((1, 2 * channels), F32),
        ((2 * channels, 2 * hidden), BF16),
        ((1, 2 * hidden), F32),
        ((2 * hidden, 2 * channels), BF16),
        ((1, 2 * channels), F32),
        ((2 * channels, 2 * channels), BF16),
        ((count, HEAD), F32),
        ((count, HEAD), F32),
        ((count, count), F32),
    ]
    return pl.pallas_call(
        prepare_kernel,
        out_shape=[jax.ShapeDtypeStruct(*s) for s in shapes],
        in_specs=[in_smem()] * 4 + [in_vmem()] * 7,
        out_specs=[in_vmem()] * len(shapes),
        compiler_params=pltpu.CompilerParams(vmem_limit_bytes=VMEM_LIMIT),
        cost_estimate=pl.CostEstimate(
            flops=10_000_000, bytes_accessed=4_000_000, transcendentals=100_000
        ),
    )(place, *chains, pair_weight, *vectors)


def body(
    tokens,
    query_weight,
    key_weight,
    old_maps,
    pair_weight,
    pair_bias,
    norm_gain,
    norm_bias,
    hidden_weight,
    hidden_bias,
    out_weight,
    out_bias,
    chain_starts,
    chain_lengths,
    chain_groups,
    tile_owner,
):
    row_count = lax.axis_size(DP)
    column_count = lax.axis_size(COL)
    bin_tokens = tokens.shape[0]
    block_width = bin_tokens // column_count
    place = jnp.stack([lax.axis_index(a) for a in ("x", "z", "y", "k")])
    place = place.astype(jnp.int32)

    q_left, q_right = gathered_rows(query_weight)
    k_left, k_right = gathered_rows(key_weight)
    older = older_part(0, old_maps, pair_weight)
    q_left, k_right, older = lax.optimization_barrier((q_left, k_right, older))
    q_far = shifted(q_left, "x", 1)
    k_far = shifted(k_right, "x", -1)
    blocks = token_blocks(tokens)
    older = older_part(1, old_maps, pair_weight, older)
    blocks, older = lax.optimization_barrier((blocks, older))
    tok = turn(place, blocks)
    partial = project(
        tok, (query_weight, q_left, q_right, q_far, key_weight, k_left, k_right, k_far)
    )
    partial, chains = lax.optimization_barrier(
        (partial, (chain_starts, chain_lengths, chain_groups))
    )
    row = lambda a: a.reshape(1, -1)
    prepared = prepare(
        place,
        chains,
        pair_weight,
        (
            row(norm_gain),
            row(norm_bias),
            hidden_weight,
            row(hidden_bias),
            out_weight,
            row(out_bias),
        ),
        tokens,
    )
    q_zero, k_zero, q_one, k_one, q_three, k_three, q_two, k_two = (
        partial[i] for i in (0, 1, 2, 3, 6, 7, 4, 5)
    )
    q_two = shifted(q_two, "z", 1)
    k_two = shifted(k_two, "z", -1)
    k_one = shifted(k_one, "z", 1)
    q_three = shifted(q_three, "z", -1)
    q_two, k_two, prepared = lax.optimization_barrier((q_two, k_two, prepared))
    new_weight, key_ids, query_ids = prepared[:3]
    vectors = (row(pair_bias), *prepared[3:10])
    cosine, sine, allowed = prepared[10:]
    q_one, k_three = two_sums(q_one, q_two, k_three, k_two)
    q_one = shifted(q_one, "z", 1)
    k_three = shifted(k_three, "z", -1)

    maps = attend(
        place, q_zero, q_one, q_three, k_zero, k_one, k_three, cosine, sine, allowed
    )
    places = [(y, k) for y in range(SIDE) for k in range(2)]

    def sent(by, core):
        return lax.ppermute(
            maps[core * SIDE + by % SIDE],
            COL,
            [(y * 2 + k, (y + by) % SIDE * 2 + (k + core) % 2) for y, k in places],
        )

    far = [[sent(by, core) for by in (1, -1, 2)] for core in range(2)]
    spread_maps = jnp.stack([maps[0], *far[0], sent(0, 1), *far[1]])
    by_group = spread_maps.reshape(-1, SIDE, GROUPS, 2, bin_tokens).transpose(0, 2, 1, 3, 4)
    by_group = by_group.reshape(-1, SIDE * 2 * bin_tokens)
    outgoing = refine(
        tile_owner[0, 0], row_count, older, by_group, new_weight, key_ids, query_ids, vectors
    )
    outgoing = outgoing.reshape(1, row_count, 1, *outgoing.shape[1:])
    return lax.all_to_all(outgoing, DP, split_axis=1, concat_axis=1, tiled=True)


def solution(mesh):
    split = Mesh(mesh.devices.reshape(SIDE, SIDE, SIDE, 2), ("x", "z", "y", "k"))
    placed = (
        P(DP, COL),
        P(DP, COL),
        P(DP, COL),
        P(None, DP, COL, None),
        P(),
        P(),
        P(),
        P(),
        P(),
        P(),
        P(),
        P(),
        P(DP, None),
        P(DP, None),
        P(DP, None),
        P(DP, COL, None),
    )
    return jax.shard_map(
        body, mesh=split, in_specs=placed, out_specs=P(DP, None, COL, None, None), check_vma=False
    )
```

```python
import math

import jax
import jax.numpy as jnp
from jax import lax
from jax.experimental import pallas as pl
from jax.experimental.pallas import tpu as pltpu
from jax.sharding import Mesh
from jax.sharding import PartitionSpec as P

HEAD = 128
DP = ("x", "z")
COL = ("y", "k")
SIDE = 4
STEPS = 1
BATCH = 2
PIECE_SHIFTS = (0, 3, 1, 2)
VMEM_LIMIT = 28 * 1024 * 1024
BF16 = jnp.bfloat16
F32 = jnp.float32


def shifted(value, axis, by):
    return lax.ppermute(value, axis, [(i, (i + by) % SIDE) for i in range(SIDE)])


def in_vmem():
    return pl.BlockSpec(memory_space=pltpu.VMEM)


def in_smem():
    return pl.BlockSpec(memory_space=pltpu.SMEM)


def token_blocks(tokens):
    turned = tokens.T
    half = turned.shape[0] // 2
    z = lax.axis_index("z")
    halves = turned.reshape(2, half, turned.shape[1])
    near = lax.dynamic_index_in_dim(halves, z // 2, 0, keepdims=False)
    far = lax.dynamic_index_in_dim(halves, 1 - z // 2, 0, keepdims=False)
    pairs = [(s, c) for s in range(SIDE) for c in range(2)]
    first = lax.ppermute(
        near, ("z", "k"), [(s * 2 + c, (2 * c + s // 2) * 2 + s % 2) for s, c in pairs]
    )
    second = lax.ppermute(
        far, ("z", "k"), [(s * 2 + c, (2 * c + 1 - s // 2) * 2 + s % 2) for s, c in pairs]
    )
    even = z % 2 == 0
    mine = jnp.stack([jnp.where(even, first, second), jnp.where(even, second, first)])
    filled = lax.all_gather(mine, COL, axis=0, tiled=False)
    return filled.reshape(SIDE, 2, *mine.shape)


def gathered_rows(weight):
    return shifted(weight, "x", 1), shifted(weight, "x", -1)


def turn_kernel(place, blocks, out):
    x, z = place[0], place[1]
    rows, width = blocks.shape[-2:]
    for j in range(SIDE):
        source = lax.rem(z + j, SIDE)
        pieces = [
            blocks[lax.rem(x + shift, SIDE), lax.rem(source, 2), source // 2]
            for shift in PIECE_SHIFTS
        ]
        out[width * j : width * (j + 1), :] = jnp.concatenate(pieces, axis=0).T


def turn(place, blocks):
    rows, width = blocks.shape[-2:]
    return pl.pallas_call(
        turn_kernel,
        out_shape=jax.ShapeDtypeStruct((SIDE * width, SIDE * rows), BF16),
        in_specs=[in_smem(), in_vmem()],
        out_specs=in_vmem(),
        compiler_params=pltpu.CompilerParams(vmem_limit_bytes=VMEM_LIMIT),
        cost_estimate=pl.CostEstimate(flops=0, bytes_accessed=8_000_000, transcendentals=0),
    )(place, blocks)


def project_kernel(tok, *refs):
    pieces, outs, wgt = refs[:8], refs[8:16], refs[16]
    rows, columns = pieces[0].shape
    width = outs[0].shape[0]
    for part in range(2):
        for at in range(SIDE):
            wgt[rows * at : rows * (at + 1), columns * part : columns * (part + 1)] = pieces[
                SIDE * part + at
            ][...]
    whole = jnp.dot(tok[...], wgt[...], preferred_element_type=F32).astype(BF16)
    for j in range(SIDE):
        for part in range(2):
            outs[2 * j + part][...] = whole[
                width * j : width * (j + 1), columns * part : columns * (part + 1)
            ]


def project(tok, pieces):
    rows, columns = pieces[0].shape
    total = tok.shape[0]
    return pl.pallas_call(
        project_kernel,
        out_shape=[jax.ShapeDtypeStruct((total // SIDE, columns), BF16)] * 8,
        in_specs=[in_vmem()] * 9,
        out_specs=[in_vmem()] * 8,
        scratch_shapes=[pltpu.VMEM((SIDE * rows, 2 * columns), BF16)],
        compiler_params=pltpu.CompilerParams(vmem_limit_bytes=VMEM_LIMIT),
        cost_estimate=pl.CostEstimate(
            flops=2 * SIDE * rows * total * 2 * columns,
            bytes_accessed=10_000_000,
            transcendentals=0,
        ),
    )(tok, *pieces)


def add_kernel(a, b, c, d, first, second):
    first[...] = (a[...].astype(F32) + b[...].astype(F32)).astype(BF16)
    second[...] = (c[...].astype(F32) + d[...].astype(F32)).astype(BF16)


def two_sums(a, b, c, d):
    shape = jax.ShapeDtypeStruct(a.shape, a.dtype)
    return pl.pallas_call(
        add_kernel,
        out_shape=[shape] * 2,
        in_specs=[in_vmem()] * 4,
        out_specs=[in_vmem()] * 2,
        cost_estimate=pl.CostEstimate(flops=a.size * 2, bytes_accessed=2_000_000, transcendentals=0),
    )(a, b, c, d)


def attend_kernel(place, starts, lengths, groups, q0, q1, q3, k0, k1, k3, *outs):
    *outs, held = outs
    heads = q0.shape[1] // HEAD
    cores, sides = 2, len(outs) // 2
    keys = q0.shape[0] // (cores * sides)
    scale = 1.0 / math.sqrt(HEAD)
    tokens = q0.shape[0]
    square = (tokens, tokens)
    rows, columns = iota(square, 0), iota(square, 1)
    same = (
        described(rows, -1, starts, lengths, groups)[0]
        == described(columns, -2, starts, lengths, groups)[0]
    )
    keep = same | (rows == columns)
    half = HEAD // 2
    lane = iota((tokens, HEAD), 1)
    offset = described(iota((tokens, HEAD), 0), -1, starts, lengths, groups)[1]
    frequency = jnp.exp(lax.rem(lane, half).astype(F32) * (-2.0 * math.log(10000.0) / HEAD))
    angles = offset.astype(F32) * frequency
    cos = jnp.cos(angles)
    sin = jnp.where(lane < half, -jnp.sin(angles), jnp.sin(angles))

    def turned(parts, h):
        cols = pl.ds(h * HEAD, HEAD)
        own, left, right = parts
        whole = own[:, cols].astype(F32) + left[:, cols].astype(F32) + right[:, cols].astype(F32)
        return (whole * cos + pltpu.roll(whole, HEAD // 2, 1) * sin).astype(BF16)

    for h in range(heads):
        query = turned((q0, q1, q3), h)
        key = turned((k0, k1, k3), h)
        scores = (
            lax.dot_general(key, query, (((1,), (1,)), ((), ())), preferred_element_type=F32)
            * scale
        )
        masked = jnp.where(keep, scores, -1e30)
        largest = jnp.max(masked, axis=0, keepdims=True)
        powers = jnp.exp(masked - largest)
        held[...] = (powers / jnp.sum(powers, axis=0, keepdims=True)).astype(BF16)
        for side in range(sides):
            for core in range(cores):
                block = lax.rem(place[2] + side, sides) * cores + lax.rem(place[3] + core, cores)
                mine = pl.ds(pl.multiple_of(block * keys, keys), keys)
                outs[core * sides + side][h] = held[mine, :]


def attend(place, chains, *operands):
    width, columns = operands[0].shape
    heads = columns // HEAD
    return pl.pallas_call(
        attend_kernel,
        out_shape=[jax.ShapeDtypeStruct((heads, width // 8, width), BF16)] * (2 * SIDE),
        in_specs=[in_smem()] * 4 + [in_vmem()] * 6,
        out_specs=[in_vmem()] * (2 * SIDE),
        scratch_shapes=[pltpu.VMEM((width, width), BF16)],
        compiler_params=pltpu.CompilerParams(vmem_limit_bytes=VMEM_LIMIT),
        cost_estimate=pl.CostEstimate(
            flops=2 * heads * HEAD * width * width,
            bytes_accessed=3_000_000,
            transcendentals=heads * width * width,
        ),
    )(place, *chains, *operands)


def older_kernel(maps, weight, *refs):
    out = refs[-1]
    turned = weight[: maps.shape[0], :].T
    by_key = jnp.swapaxes(maps[:, 0], 0, 1)
    for u in range(maps.shape[2]):
        out[u] = jnp.dot(turned, by_key[u], preferred_element_type=F32).T.astype(BF16)


def older_part(half, maps, weight, before=None):
    depth, _, keys, queries = maps.shape
    channels = weight.shape[1]
    some = keys // 2
    extra = () if before is None else (before,)
    return pl.pallas_call(
        older_kernel,
        out_shape=jax.ShapeDtypeStruct((keys, queries, channels), BF16),
        grid=(1,),
        in_specs=[
            pl.BlockSpec((depth, 1, some, queries), lambda i: (0, 0, half, 0)),
            pl.BlockSpec(weight.shape, lambda i: (0, 0)),
        ]
        + [pl.BlockSpec(memory_space=pl.ANY)] * len(extra),
        out_specs=pl.BlockSpec((some, queries, channels), lambda i: (half, 0, 0)),
        input_output_aliases={2: 0} if extra else {},
        compiler_params=pltpu.CompilerParams(vmem_limit_bytes=40 * 1024 * 1024),
        cost_estimate=pl.CostEstimate(
            flops=2 * depth * some * queries * channels,
            bytes_accessed=2 * depth * some * queries,
            transcendentals=0,
        ),
    )(maps, weight, *extra)


def described(places, outside, starts, lengths, groups):
    ids = jnp.full(places.shape, outside, jnp.int32)
    offset = jnp.zeros(places.shape, jnp.int32)
    for c in range(starts.shape[1]):
        first = starts[0, c]
        member = (places >= first) & (places < first + lengths[0, c])
        ids = jnp.where(member, groups[0, c], ids)
        offset = jnp.where(member, places - first, offset)
    return ids, offset


def iota(shape, dim):
    return lax.broadcasted_iota(jnp.int32, shape, dim)


def refine_kernel(owners, place, starts, lengths, groups, older, *refs):
    maps, refs = refs[: 2 * SIDE], refs[2 * SIDE :]
    (pair_weight, pair_bias, gain, norm_bias, hidden_weight, hidden_bias, out_weight) = refs[:7]
    out_bias, out = refs[7:9]
    (by_key, new_weight, hidden_two, out_two, ones, query_ids, key_ids) = refs[9:16]
    zeros, staged, zero_sems, tile_sems = refs[16:]
    step = pl.program_id(0)
    keys, queries, channels = older.shape
    hidden_width = hidden_bias.shape[1]
    count = out.shape[0]
    tiles = owners.shape[0]
    tile = queries // tiles

    def empty(o):
        none = owners[0] != o
        for i in range(1, tiles):
            none = none & (owners[i] != o)
        return none

    def blank(o):
        return pltpu.make_async_copy(zeros, out.at[o], zero_sems.at[o])

    def sent(r):
        some = pl.ds(pl.multiple_of(step * keys * tile, keys * tile), keys * tile)
        return pltpu.make_async_copy(
            staged.at[r, some], out.at[owners[r], some], tile_sems.at[step, r]
        )

    @pl.when(step == 0)
    def _():
        zeros[...] = jnp.zeros_like(zeros)
        for o in range(count):

            @pl.when(empty(o))
            def _(o=o):
                blank(o).start()

        by_key[...] = jnp.swapaxes(jnp.concatenate([m[...] for m in maps], axis=0), 0, 1)
        heads_all = by_key.shape[1]
        per_core = heads_all // (2 * SIDE)
        shape = (heads_all, heads_all)
        at = iota(shape, 1)
        piece = lax.rem(at // per_core, SIDE)
        shift = jnp.where(piece == 1, 3, jnp.where(piece == 2, 1, jnp.where(piece == 3, 2, 0)))
        core = lax.rem(at // (per_core * SIDE) + place[3], 2)
        side = lax.rem(place[2] + shift, SIDE)
        head = (side * 2 + core) * per_core + lax.rem(at, per_core)
        chosen = jnp.where(iota(shape, 0) == head, 1.0, 0.0).astype(BF16)
        old = pair_weight.shape[0] - heads_all
        new_weight[...] = lax.dot_general(
            pair_weight[old:, :], chosen, (((0,), (0,)), ((), ())), preferred_element_type=F32
        ).astype(BF16)
        query_ids[...] = described(iota(query_ids.shape, 0), -1, starts, lengths, groups)[
            0
        ].astype(F32)
        first_key = (place[2] * 2 + place[3]) * key_ids.shape[0]
        key_ids[...] = described(
            iota(key_ids.shape, 0) + first_key, -2, starts, lengths, groups
        )[0].astype(F32)
        shape = ones.shape
        ones[...] = jnp.where(
            iota(shape, 0) // channels == iota(shape, 1) // channels, 1.0, 0.0
        ).astype(BF16)
        hidden_two[...] = jnp.zeros_like(hidden_two)
        hidden_two[:channels, :hidden_width] = hidden_weight[...]
        hidden_two[channels:, hidden_width:] = hidden_weight[...]
        out_two[...] = jnp.zeros_like(out_two)
        out_two[:hidden_width, :channels] = out_weight[...]
        out_two[hidden_width:, channels:] = out_weight[...]

    twice = lambda ref: jnp.concatenate([ref[...], ref[...]], axis=1)
    gain_two, norm_two, hbias_two, obias_two = (
        twice(ref) for ref in (gain, norm_bias, hidden_bias, out_bias)
    )

    def pair_of(e):
        fresh = jnp.dot(new_weight[...], by_key[step * keys + e], preferred_element_type=F32).T
        return older[e].astype(F32) + fresh + pair_bias[...]

    span = 2 * BATCH
    for base in range(0, keys, 2 * span):
        pair = jnp.concatenate(
            [
                jnp.concatenate([pair_of(base + span * side + e) for e in range(span)], axis=0)
                for side in range(2)
            ],
            axis=1,
        ).astype(BF16)
        values = pair.astype(F32)
        mean = jnp.dot(pair, ones[...], preferred_element_type=F32) * (1.0 / channels)
        centred = values - mean
        spread = jnp.dot(
            (centred * centred).astype(BF16), ones[...], preferred_element_type=F32
        ) * (1.0 / channels)
        normed = (centred * lax.rsqrt(spread + 1e-05) * gain_two + norm_two).astype(BF16)
        hidden = jnp.maximum(
            jnp.dot(normed, hidden_two[...], preferred_element_type=F32) + hbias_two, 0.0
        ).astype(BF16)
        update = jnp.dot(hidden, out_two[...], preferred_element_type=F32) + obias_two
        result = values + update
        for side in range(2):
            for e in range(span):
                u = step * keys + base + span * side + e
                piece = result[
                    e * queries : (e + 1) * queries, side * channels : (side + 1) * channels
                ]
                same = key_ids[pl.ds(u, 1), :] == query_ids[...]
                piece = jnp.where(same, piece, 0.0).astype(BF16)
                at = pl.ds(pl.multiple_of(u * tile, tile), tile)
                for r in range(tiles):
                    staged[r, at, :] = piece[r * tile : (r + 1) * tile]

    for r in range(tiles):

        @pl.when(owners[r] >= 0)
        def _(r=r):
            sent(r).start()

    @pl.when(step == pl.num_programs(0) - 1)
    def _():
        for r in range(tiles):

            @pl.when(owners[r] >= 0)
            def _(r=r):
                for s in range(STEPS):
                    some = pl.ds(s * keys * tile, keys * tile)
                    pltpu.make_async_copy(
                        staged.at[r, some], out.at[owners[r], some], tile_sems.at[s, r]
                    ).wait()

        for o in range(count):

            @pl.when(empty(o))
            def _(o=o):
                blank(o).wait()


def refine(owners, count, place, chains, older, maps, weights):
    keys, queries, channels = older.shape
    tiles = owners.shape[0]
    tile_pairs = keys * queries // tiles
    hidden = weights[4].shape[1]
    heads_all = sum(m.shape[0] for m in maps)
    whole = lambda a: pl.BlockSpec(a.shape, lambda i, n=a.ndim: (0,) * n)
    return pl.pallas_call(
        refine_kernel,
        out_shape=jax.ShapeDtypeStruct((count, tile_pairs, channels), BF16),
        grid=(STEPS,),
        in_specs=[in_smem()] * 5
        + [pl.BlockSpec((keys // STEPS, queries, channels), lambda i: (i, 0, 0))]
        + [whole(a) for a in (*maps, *weights)],
        out_specs=pl.BlockSpec(memory_space=pl.ANY),
        scratch_shapes=[
            pltpu.VMEM((keys, heads_all, queries), BF16),
            pltpu.VMEM((channels, heads_all), BF16),
            pltpu.VMEM((2 * channels, 2 * hidden), BF16),
            pltpu.VMEM((2 * hidden, 2 * channels), BF16),
            pltpu.VMEM((2 * channels, 2 * channels), BF16),
            pltpu.VMEM((queries, channels), F32),
            pltpu.VMEM((keys, channels), F32),
            pltpu.VMEM((tile_pairs, channels), BF16),
            pltpu.VMEM((tiles, tile_pairs, channels), BF16),
            pltpu.SemaphoreType.DMA((count,)),
            pltpu.SemaphoreType.DMA((STEPS, tiles)),
        ],
        compiler_params=pltpu.CompilerParams(vmem_limit_bytes=VMEM_LIMIT),
        cost_estimate=pl.CostEstimate(
            flops=4 * keys * queries * channels * 640,
            bytes_accessed=10_000_000,
            transcendentals=0,
        ),
    )(owners, place, *chains, older, *maps, *weights)


def body(
    tokens,
    query_weight,
    key_weight,
    old_maps,
    pair_weight,
    pair_bias,
    norm_gain,
    norm_bias,
    hidden_weight,
    hidden_bias,
    out_weight,
    out_bias,
    chain_starts,
    chain_lengths,
    chain_groups,
    tile_owner,
):
    row_count = lax.axis_size(DP)
    bin_tokens = tokens.shape[0]
    place = jnp.stack([lax.axis_index(a) for a in ("x", "z", "y", "k")])
    place = place.astype(jnp.int32)

    q_left, q_right = gathered_rows(query_weight)
    k_left, k_right = gathered_rows(key_weight)
    older = older_part(0, old_maps, pair_weight)
    q_left, k_right, older = lax.optimization_barrier((q_left, k_right, older))
    q_far = shifted(q_left, "x", 1)
    k_far = shifted(k_right, "x", -1)
    blocks = token_blocks(tokens)
    older = older_part(1, old_maps, pair_weight, older)
    blocks, older = lax.optimization_barrier((blocks, older))
    tok = turn(place, blocks)
    partial = project(
        tok, (query_weight, q_left, q_right, q_far, key_weight, k_left, k_right, k_far)
    )
    chains = (chain_starts, chain_lengths, chain_groups)
    row = lambda a: a.reshape(1, -1)
    q_zero, k_zero, q_one, k_one, q_three, k_three, q_two, k_two = (
        partial[i] for i in (0, 1, 2, 3, 6, 7, 4, 5)
    )
    q_two = shifted(q_two, "z", 1)
    k_two = shifted(k_two, "z", -1)
    k_one = shifted(k_one, "z", 1)
    q_three = shifted(q_three, "z", -1)
    q_one, k_three = two_sums(q_one, q_two, k_three, k_two)
    q_one = shifted(q_one, "z", 1)
    k_three = shifted(k_three, "z", -1)

    maps = attend(place, chains, q_zero, q_one, q_three, k_zero, k_one, k_three)
    places = [(y, k) for y in range(SIDE) for k in range(2)]

    def sent(by, core):
        return lax.ppermute(
            maps[core * SIDE + by % SIDE],
            COL,
            [(y * 2 + k, (y + by) % SIDE * 2 + (k + core) % 2) for y, k in places],
        )

    far = [[sent(by, core) for by in (1, -1, 2)] for core in range(2)]
    outgoing = refine(
        tile_owner[0, 0],
        row_count,
        place,
        chains,
        older,
        (maps[0], *far[0], sent(0, 1), *far[1]),
        (
            pair_weight,
            row(pair_bias),
            row(norm_gain),
            row(norm_bias),
            hidden_weight,
            row(hidden_bias),
            out_weight,
            row(out_bias),
        ),
    )
    outgoing = outgoing.reshape(1, row_count, 1, *outgoing.shape[1:])
    return lax.all_to_all(outgoing, DP, split_axis=1, concat_axis=1, tiled=True)


def solution(mesh):
    split = Mesh(mesh.devices.reshape(SIDE, SIDE, SIDE, 2), ("x", "z", "y", "k"))
    placed = (
        P(DP, COL),
        P(DP, COL),
        P(DP, COL),
        P(None, DP, COL, None),
        P(),
        P(),
        P(),
        P(),
        P(),
        P(),
        P(),
        P(),
        P(DP, None),
        P(DP, None),
        P(DP, None),
        P(DP, COL, None),
    )
    return jax.shard_map(
        body, mesh=split, in_specs=placed, out_specs=P(DP, None, COL, None, None), check_vma=False
    )
```

```python
import math

import jax
import jax.numpy as jnp
from jax import lax
from jax.experimental import pallas as pl
from jax.experimental.pallas import tpu as pltpu
from jax.sharding import Mesh
from jax.sharding import PartitionSpec as P

HEAD = 128
DP = ("x", "z")
COL = ("y", "k")
SIDE = 4
STEPS = 1
BATCH = 2
PIECE_SHIFTS = (0, 3, 1, 2)
VMEM_LIMIT = 28 * 1024 * 1024
BF16 = jnp.bfloat16
F32 = jnp.float32


def shifted(value, axis, by):
    return lax.ppermute(value, axis, [(i, (i + by) % SIDE) for i in range(SIDE)])


def in_vmem():
    return pl.BlockSpec(memory_space=pltpu.VMEM)


def in_smem():
    return pl.BlockSpec(memory_space=pltpu.SMEM)


def token_blocks(tokens):
    turned = tokens.T
    half = turned.shape[0] // 2
    z = lax.axis_index("z")
    halves = turned.reshape(2, half, turned.shape[1])
    near = lax.dynamic_index_in_dim(halves, z // 2, 0, keepdims=False)
    far = lax.dynamic_index_in_dim(halves, 1 - z // 2, 0, keepdims=False)
    pairs = [(s, c) for s in range(SIDE) for c in range(2)]
    first = lax.ppermute(
        near, ("z", "k"), [(s * 2 + c, (2 * c + s // 2) * 2 + s % 2) for s, c in pairs]
    )
    second = lax.ppermute(
        far, ("z", "k"), [(s * 2 + c, (2 * c + 1 - s // 2) * 2 + s % 2) for s, c in pairs]
    )
    even = z % 2 == 0
    mine = jnp.stack([jnp.where(even, first, second), jnp.where(even, second, first)])
    filled = lax.all_gather(mine, COL, axis=0, tiled=False)
    return filled.reshape(SIDE, 2, *mine.shape)


def gathered_rows(weight):
    return shifted(weight, "x", 1), shifted(weight, "x", -1)


def turn_kernel(place, blocks, out):
    x, z = place[0], place[1]
    rows, width = blocks.shape[-2:]
    for j in range(SIDE):
        source = lax.rem(z + j, SIDE)
        pieces = [
            blocks[lax.rem(x + shift, SIDE), lax.rem(source, 2), source // 2]
            for shift in PIECE_SHIFTS
        ]
        out[width * j : width * (j + 1), :] = jnp.concatenate(pieces, axis=0).T


def turn(place, blocks):
    rows, width = blocks.shape[-2:]
    return pl.pallas_call(
        turn_kernel,
        out_shape=jax.ShapeDtypeStruct((SIDE * width, SIDE * rows), BF16),
        in_specs=[in_smem(), in_vmem()],
        out_specs=in_vmem(),
        compiler_params=pltpu.CompilerParams(vmem_limit_bytes=VMEM_LIMIT),
        cost_estimate=pl.CostEstimate(flops=0, bytes_accessed=8_000_000, transcendentals=0),
    )(place, blocks)


def project_kernel(tok, *refs):
    pieces, outs, wgt = refs[:8], refs[8:16], refs[16]
    rows, columns = pieces[0].shape
    width = outs[0].shape[0]
    for part in range(2):
        for at in range(SIDE):
            wgt[rows * at : rows * (at + 1), columns * part : columns * (part + 1)] = pieces[
                SIDE * part + at
            ][...]
    whole = jnp.dot(tok[...], wgt[...], preferred_element_type=F32).astype(BF16)
    for j in range(SIDE):
        for part in range(2):
            outs[2 * j + part][...] = whole[
                width * j : width * (j + 1), columns * part : columns * (part + 1)
            ]


def project(tok, pieces):
    rows, columns = pieces[0].shape
    total = tok.shape[0]
    return pl.pallas_call(
        project_kernel,
        out_shape=[jax.ShapeDtypeStruct((total // SIDE, columns), BF16)] * 8,
        in_specs=[in_vmem()] * 9,
        out_specs=[in_vmem()] * 8,
        scratch_shapes=[pltpu.VMEM((SIDE * rows, 2 * columns), BF16)],
        compiler_params=pltpu.CompilerParams(vmem_limit_bytes=VMEM_LIMIT),
        cost_estimate=pl.CostEstimate(
            flops=2 * SIDE * rows * total * 2 * columns,
            bytes_accessed=10_000_000,
            transcendentals=0,
        ),
    )(tok, *pieces)


def add_kernel(a, b, c, d, first, second):
    first[...] = (a[...].astype(F32) + b[...].astype(F32)).astype(BF16)
    second[...] = (c[...].astype(F32) + d[...].astype(F32)).astype(BF16)


def two_sums(a, b, c, d):
    shape = jax.ShapeDtypeStruct(a.shape, a.dtype)
    return pl.pallas_call(
        add_kernel,
        out_shape=[shape] * 2,
        in_specs=[in_vmem()] * 4,
        out_specs=[in_vmem()] * 2,
        cost_estimate=pl.CostEstimate(flops=a.size * 2, bytes_accessed=2_000_000, transcendentals=0),
    )(a, b, c, d)


def attend_kernel(place, starts, lengths, groups, q0, q1, q3, k0, k1, k3, *outs):
    *outs, held = outs
    heads = q0.shape[1] // HEAD
    cores, sides = 2, len(outs)
    keys = q0.shape[0] // (cores * sides)
    scale = 1.0 / math.sqrt(HEAD)
    tokens = q0.shape[0]
    square = (tokens, tokens)
    rows, columns = iota(square, 0), iota(square, 1)
    same = (
        described(rows, -1, starts, lengths, groups)[0]
        == described(columns, -2, starts, lengths, groups)[0]
    )
    keep = same | (rows == columns)
    half = HEAD // 2
    lane = iota((tokens, HEAD), 1)
    offset = described(iota((tokens, HEAD), 0), -1, starts, lengths, groups)[1]
    frequency = jnp.exp(lax.rem(lane, half).astype(F32) * (-2.0 * math.log(10000.0) / HEAD))
    angles = offset.astype(F32) * frequency
    cos = jnp.cos(angles)
    sin = jnp.where(lane < half, -jnp.sin(angles), jnp.sin(angles))

    def turned(parts, h):
        cols = pl.ds(h * HEAD, HEAD)
        own, left, right = parts
        whole = own[:, cols].astype(F32) + left[:, cols].astype(F32) + right[:, cols].astype(F32)
        return (whole * cos + pltpu.roll(whole, HEAD // 2, 1) * sin).astype(BF16)

    for h in range(heads):
        query = turned((q0, q1, q3), h)
        key = turned((k0, k1, k3), h)
        scores = (
            lax.dot_general(key, query, (((1,), (1,)), ((), ())), preferred_element_type=F32)
            * scale
        )
        masked = jnp.where(keep, scores, -1e30)
        largest = jnp.max(masked, axis=0, keepdims=True)
        powers = jnp.exp(masked - largest)
        held[...] = (powers / jnp.sum(powers, axis=0, keepdims=True)).astype(BF16)
        for side in range(sides):
            for core in range(cores):
                block = lax.rem(place[2] + side, sides) * cores + lax.rem(place[3] + core, cores)
                mine = pl.ds(pl.multiple_of(block * keys, keys), keys)
                outs[side][core, h] = held[mine, :]


def attend(place, chains, *operands):
    width, columns = operands[0].shape
    heads = columns // HEAD
    return pl.pallas_call(
        attend_kernel,
        out_shape=[jax.ShapeDtypeStruct((2, heads, width // 8, width), BF16)] * SIDE,
        in_specs=[in_smem()] * 4 + [in_vmem()] * 6,
        out_specs=[in_vmem()] * SIDE,
        scratch_shapes=[pltpu.VMEM((width, width), BF16)],
        compiler_params=pltpu.CompilerParams(vmem_limit_bytes=VMEM_LIMIT),
        cost_estimate=pl.CostEstimate(
            flops=2 * heads * HEAD * width * width,
            bytes_accessed=3_000_000,
            transcendentals=heads * width * width,
        ),
    )(place, *chains, *operands)


def older_kernel(maps, weight, *refs):
    out = refs[-1]
    turned = weight[: maps.shape[0], :].T
    by_key = jnp.swapaxes(maps[:, 0], 0, 1)
    for u in range(maps.shape[2]):
        out[u] = jnp.dot(turned, by_key[u], preferred_element_type=F32).T.astype(BF16)


def older_part(half, maps, weight, before=None):
    depth, _, keys, queries = maps.shape
    channels = weight.shape[1]
    some = keys // 2
    extra = () if before is None else (before,)
    return pl.pallas_call(
        older_kernel,
        out_shape=jax.ShapeDtypeStruct((keys, queries, channels), BF16),
        grid=(1,),
        in_specs=[
            pl.BlockSpec((depth, 1, some, queries), lambda i: (0, 0, half, 0)),
            pl.BlockSpec(weight.shape, lambda i: (0, 0)),
        ]
        + [pl.BlockSpec(memory_space=pl.ANY)] * len(extra),
        out_specs=pl.BlockSpec((some, queries, channels), lambda i: (half, 0, 0)),
        input_output_aliases={2: 0} if extra else {},
        compiler_params=pltpu.CompilerParams(vmem_limit_bytes=40 * 1024 * 1024),
        cost_estimate=pl.CostEstimate(
            flops=2 * depth * some * queries * channels,
            bytes_accessed=2 * depth * some * queries,
            transcendentals=0,
        ),
    )(maps, weight, *extra)


def described(places, outside, starts, lengths, groups):
    ids = jnp.full(places.shape, outside, jnp.int32)
    offset = jnp.zeros(places.shape, jnp.int32)
    for c in range(starts.shape[1]):
        first = starts[0, c]
        member = (places >= first) & (places < first + lengths[0, c])
        ids = jnp.where(member, groups[0, c], ids)
        offset = jnp.where(member, places - first, offset)
    return ids, offset


def iota(shape, dim):
    return lax.broadcasted_iota(jnp.int32, shape, dim)


def refine_kernel(owners, place, starts, lengths, groups, older, *refs):
    maps, refs = refs[: SIDE + 1], refs[SIDE + 1 :]
    (pair_weight, pair_bias, gain, norm_bias, hidden_weight, hidden_bias, out_weight) = refs[:7]
    out_bias, out = refs[7:9]
    (by_key, new_weight, hidden_two, out_two, ones, query_ids, key_ids) = refs[9:16]
    zeros, staged, zero_sems, tile_sems = refs[16:]
    step = pl.program_id(0)
    keys, queries, channels = older.shape
    hidden_width = hidden_bias.shape[1]
    count = out.shape[0]
    tiles = owners.shape[0]
    tile = queries // tiles

    def empty(o):
        none = owners[0] != o
        for i in range(1, tiles):
            none = none & (owners[i] != o)
        return none

    def blank(o):
        return pltpu.make_async_copy(zeros, out.at[o], zero_sems.at[o])

    def sent(r):
        some = pl.ds(pl.multiple_of(step * keys * tile, keys * tile), keys * tile)
        return pltpu.make_async_copy(
            staged.at[r, some], out.at[owners[r], some], tile_sems.at[step, r]
        )

    @pl.when(step == 0)
    def _():
        zeros[...] = jnp.zeros_like(zeros)
        for o in range(count):

            @pl.when(empty(o))
            def _(o=o):
                blank(o).start()

        parts = [m[0] for m in maps[:SIDE]] + [maps[SIDE][i] for i in range(SIDE)]
        by_key[...] = jnp.swapaxes(jnp.concatenate(parts, axis=0), 0, 1)
        heads_all = by_key.shape[1]
        per_core = heads_all // (2 * SIDE)
        shape = (heads_all, heads_all)
        at = iota(shape, 1)
        piece = lax.rem(at // per_core, SIDE)
        shift = jnp.where(piece == 1, 3, jnp.where(piece == 2, 1, jnp.where(piece == 3, 2, 0)))
        core = lax.rem(at // (per_core * SIDE) + place[3], 2)
        side = lax.rem(place[2] + shift, SIDE)
        head = (side * 2 + core) * per_core + lax.rem(at, per_core)
        chosen = jnp.where(iota(shape, 0) == head, 1.0, 0.0).astype(BF16)
        old = pair_weight.shape[0] - heads_all
        new_weight[...] = lax.dot_general(
            pair_weight[old:, :], chosen, (((0,), (0,)), ((), ())), preferred_element_type=F32
        ).astype(BF16)
        query_ids[...] = described(iota(query_ids.shape, 0), -1, starts, lengths, groups)[
            0
        ].astype(F32)
        first_key = (place[2] * 2 + place[3]) * key_ids.shape[0]
        key_ids[...] = described(
            iota(key_ids.shape, 0) + first_key, -2, starts, lengths, groups
        )[0].astype(F32)
        shape = ones.shape
        ones[...] = jnp.where(
            iota(shape, 0) // channels == iota(shape, 1) // channels, 1.0, 0.0
        ).astype(BF16)
        hidden_two[...] = jnp.zeros_like(hidden_two)
        hidden_two[:channels, :hidden_width] = hidden_weight[...]
        hidden_two[channels:, hidden_width:] = hidden_weight[...]
        out_two[...] = jnp.zeros_like(out_two)
        out_two[:hidden_width, :channels] = out_weight[...]
        out_two[hidden_width:, channels:] = out_weight[...]

    twice = lambda ref: jnp.concatenate([ref[...], ref[...]], axis=1)
    gain_two, norm_two, hbias_two, obias_two = (
        twice(ref) for ref in (gain, norm_bias, hidden_bias, out_bias)
    )

    def pair_of(e):
        fresh = jnp.dot(new_weight[...], by_key[step * keys + e], preferred_element_type=F32).T
        return older[e].astype(F32) + fresh + pair_bias[...]

    span = 2 * BATCH
    for base in range(0, keys, 2 * span):
        pair = jnp.concatenate(
            [
                jnp.concatenate([pair_of(base + span * side + e) for e in range(span)], axis=0)
                for side in range(2)
            ],
            axis=1,
        ).astype(BF16)
        values = pair.astype(F32)
        mean = jnp.dot(pair, ones[...], preferred_element_type=F32) * (1.0 / channels)
        centred = values - mean
        spread = jnp.dot(
            (centred * centred).astype(BF16), ones[...], preferred_element_type=F32
        ) * (1.0 / channels)
        normed = (centred * lax.rsqrt(spread + 1e-05) * gain_two + norm_two).astype(BF16)
        hidden = jnp.maximum(
            jnp.dot(normed, hidden_two[...], preferred_element_type=F32) + hbias_two, 0.0
        ).astype(BF16)
        update = jnp.dot(hidden, out_two[...], preferred_element_type=F32) + obias_two
        result = values + update
        for side in range(2):
            for e in range(span):
                u = step * keys + base + span * side + e
                piece = result[
                    e * queries : (e + 1) * queries, side * channels : (side + 1) * channels
                ]
                same = key_ids[pl.ds(u, 1), :] == query_ids[...]
                piece = jnp.where(same, piece, 0.0).astype(BF16)
                at = pl.ds(pl.multiple_of(u * tile, tile), tile)
                for r in range(tiles):
                    staged[r, at, :] = piece[r * tile : (r + 1) * tile]

    for r in range(tiles):

        @pl.when(owners[r] >= 0)
        def _(r=r):
            sent(r).start()

    @pl.when(step == pl.num_programs(0) - 1)
    def _():
        for r in range(tiles):

            @pl.when(owners[r] >= 0)
            def _(r=r):
                for s in range(STEPS):
                    some = pl.ds(s * keys * tile, keys * tile)
                    pltpu.make_async_copy(
                        staged.at[r, some], out.at[owners[r], some], tile_sems.at[s, r]
                    ).wait()

        for o in range(count):

            @pl.when(empty(o))
            def _(o=o):
                blank(o).wait()


def refine(owners, count, place, chains, older, maps, weights):
    keys, queries, channels = older.shape
    tiles = owners.shape[0]
    tile_pairs = keys * queries // tiles
    hidden = weights[4].shape[1]
    heads_all = 2 * SIDE * maps[0].shape[1]
    whole = lambda a: pl.BlockSpec(a.shape, lambda i, n=a.ndim: (0,) * n)
    return pl.pallas_call(
        refine_kernel,
        out_shape=jax.ShapeDtypeStruct((count, tile_pairs, channels), BF16),
        grid=(STEPS,),
        in_specs=[in_smem()] * 5
        + [pl.BlockSpec((keys // STEPS, queries, channels), lambda i: (i, 0, 0))]
        + [whole(a) for a in (*maps, *weights)],
        out_specs=pl.BlockSpec(memory_space=pl.ANY),
        scratch_shapes=[
            pltpu.VMEM((keys, heads_all, queries), BF16),
            pltpu.VMEM((channels, heads_all), BF16),
            pltpu.VMEM((2 * channels, 2 * hidden), BF16),
            pltpu.VMEM((2 * hidden, 2 * channels), BF16),
            pltpu.VMEM((2 * channels, 2 * channels), BF16),
            pltpu.VMEM((queries, channels), F32),
            pltpu.VMEM((keys, channels), F32),
            pltpu.VMEM((tile_pairs, channels), BF16),
            pltpu.VMEM((tiles, tile_pairs, channels), BF16),
            pltpu.SemaphoreType.DMA((count,)),
            pltpu.SemaphoreType.DMA((STEPS, tiles)),
        ],
        compiler_params=pltpu.CompilerParams(vmem_limit_bytes=VMEM_LIMIT),
        cost_estimate=pl.CostEstimate(
            flops=4 * keys * queries * channels * 640,
            bytes_accessed=10_000_000,
            transcendentals=0,
        ),
    )(owners, place, *chains, older, *maps, *weights)


def body(
    tokens,
    query_weight,
    key_weight,
    old_maps,
    pair_weight,
    pair_bias,
    norm_gain,
    norm_bias,
    hidden_weight,
    hidden_bias,
    out_weight,
    out_bias,
    chain_starts,
    chain_lengths,
    chain_groups,
    tile_owner,
):
    row_count = lax.axis_size(DP)
    bin_tokens = tokens.shape[0]
    place = jnp.stack([lax.axis_index(a) for a in ("x", "z", "y", "k")])
    place = place.astype(jnp.int32)

    q_left, q_right = gathered_rows(query_weight)
    k_left, k_right = gathered_rows(key_weight)
    older = older_part(0, old_maps, pair_weight)
    q_left, k_right, older = lax.optimization_barrier((q_left, k_right, older))
    q_far = shifted(q_left, "x", 1)
    k_far = shifted(k_right, "x", -1)
    blocks = token_blocks(tokens)
    older = older_part(1, old_maps, pair_weight, older)
    blocks, older = lax.optimization_barrier((blocks, older))
    tok = turn(place, blocks)
    partial = project(
        tok, (query_weight, q_left, q_right, q_far, key_weight, k_left, k_right, k_far)
    )
    chains = (chain_starts, chain_lengths, chain_groups)
    row = lambda a: a.reshape(1, -1)
    q_zero, k_zero, q_one, k_one, q_three, k_three, q_two, k_two = (
        partial[i] for i in (0, 1, 2, 3, 6, 7, 4, 5)
    )
    q_two = shifted(q_two, "z", 1)
    k_two = shifted(k_two, "z", -1)
    k_one = shifted(k_one, "z", 1)
    q_three = shifted(q_three, "z", -1)
    q_one, k_three = two_sums(q_one, q_two, k_three, k_two)
    q_one = shifted(q_one, "z", 1)
    k_three = shifted(k_three, "z", -1)

    maps = attend(place, chains, q_zero, q_one, q_three, k_zero, k_one, k_three)
    pieces = [maps[0]] + [shifted(maps[by % SIDE], "y", by) for by in (1, -1, 2)]
    other = lax.ppermute(jnp.stack([p[1] for p in pieces]), "k", [(0, 1), (1, 0)])
    outgoing = refine(
        tile_owner[0, 0],
        row_count,
        place,
        chains,
        older,
        (*pieces, other),
        (
            pair_weight,
            row(pair_bias),
            row(norm_gain),
            row(norm_bias),
            hidden_weight,
            row(hidden_bias),
            out_weight,
            row(out_bias),
        ),
    )
    outgoing = outgoing.reshape(1, row_count, 1, *outgoing.shape[1:])
    return lax.all_to_all(outgoing, DP, split_axis=1, concat_axis=1, tiled=True)


def solution(mesh):
    split = Mesh(mesh.devices.reshape(SIDE, SIDE, SIDE, 2), ("x", "z", "y", "k"))
    placed = (
        P(DP, COL),
        P(DP, COL),
        P(DP, COL),
        P(None, DP, COL, None),
        P(),
        P(),
        P(),
        P(),
        P(),
        P(),
        P(),
        P(),
        P(DP, None),
        P(DP, None),
        P(DP, None),
        P(DP, COL, None),
    )
    return jax.shard_map(
        body, mesh=split, in_specs=placed, out_specs=P(DP, None, COL, None, None), check_vma=False
    )
```

```python
import math

import jax
import jax.numpy as jnp
from jax import lax
from jax.experimental import pallas as pl
from jax.experimental.pallas import tpu as pltpu
from jax.sharding import Mesh
from jax.sharding import PartitionSpec as P

HEAD = 128
DP = ("x", "z")
COL = ("y", "k")
SIDE = 4
STEPS = 1
BATCH = 2
PIECE_SHIFTS = (0, 3, 1, 2)
VMEM_LIMIT = 28 * 1024 * 1024
BF16 = jnp.bfloat16
F32 = jnp.float32


def shifted(value, axis, by):
    return lax.ppermute(value, axis, [(i, (i + by) % SIDE) for i in range(SIDE)])


def in_vmem():
    return pl.BlockSpec(memory_space=pltpu.VMEM)


def in_smem():
    return pl.BlockSpec(memory_space=pltpu.SMEM)


def token_blocks(tokens):
    turned = tokens.T
    half = turned.shape[0] // 2
    z = lax.axis_index("z")
    halves = turned.reshape(2, half, turned.shape[1])
    near = lax.dynamic_index_in_dim(halves, z // 2, 0, keepdims=False)
    far = lax.dynamic_index_in_dim(halves, 1 - z // 2, 0, keepdims=False)
    pairs = [(s, c) for s in range(SIDE) for c in range(2)]
    first = lax.ppermute(
        near, ("z", "k"), [(s * 2 + c, (2 * c + s // 2) * 2 + s % 2) for s, c in pairs]
    )
    second = lax.ppermute(
        far, ("z", "k"), [(s * 2 + c, (2 * c + 1 - s // 2) * 2 + s % 2) for s, c in pairs]
    )
    even = z % 2 == 0
    mine = jnp.stack([jnp.where(even, first, second), jnp.where(even, second, first)])
    filled = lax.all_gather(mine, COL, axis=0, tiled=False)
    return filled.reshape(SIDE, 2, *mine.shape)


def gathered_rows(weight):
    return shifted(weight, "x", 1), shifted(weight, "x", -1)


def turn_kernel(place, blocks, out):
    x, z = place[0], place[1]
    rows, width = blocks.shape[-2:]
    for j in range(SIDE):
        source = lax.rem(z + j, SIDE)
        pieces = [
            blocks[lax.rem(x + shift, SIDE), lax.rem(source, 2), source // 2]
            for shift in PIECE_SHIFTS
        ]
        out[width * j : width * (j + 1), :] = jnp.concatenate(pieces, axis=0).T


def turn(place, blocks):
    rows, width = blocks.shape[-2:]
    return pl.pallas_call(
        turn_kernel,
        out_shape=jax.ShapeDtypeStruct((SIDE * width, SIDE * rows), BF16),
        in_specs=[in_smem(), in_vmem()],
        out_specs=in_vmem(),
        compiler_params=pltpu.CompilerParams(vmem_limit_bytes=VMEM_LIMIT),
        cost_estimate=pl.CostEstimate(flops=0, bytes_accessed=8_000_000, transcendentals=0),
    )(place, blocks)


def project_kernel(tok, *refs):
    pieces, outs, wgt = refs[:8], refs[8:16], refs[16]
    rows, columns = pieces[0].shape
    width = outs[0].shape[0]
    for part in range(2):
        for at in range(SIDE):
            wgt[rows * at : rows * (at + 1), columns * part : columns * (part + 1)] = pieces[
                SIDE * part + at
            ][...]
    whole = jnp.dot(tok[...], wgt[...], preferred_element_type=F32).astype(BF16)
    for j in range(SIDE):
        for part in range(2):
            outs[2 * j + part][...] = whole[
                width * j : width * (j + 1), columns * part : columns * (part + 1)
            ]


def project(tok, pieces):
    rows, columns = pieces[0].shape
    total = tok.shape[0]
    return pl.pallas_call(
        project_kernel,
        out_shape=[jax.ShapeDtypeStruct((total // SIDE, columns), BF16)] * 8,
        in_specs=[in_vmem()] * 9,
        out_specs=[in_vmem()] * 8,
        scratch_shapes=[pltpu.VMEM((SIDE * rows, 2 * columns), BF16)],
        compiler_params=pltpu.CompilerParams(vmem_limit_bytes=VMEM_LIMIT),
        cost_estimate=pl.CostEstimate(
            flops=2 * SIDE * rows * total * 2 * columns,
            bytes_accessed=10_000_000,
            transcendentals=0,
        ),
    )(tok, *pieces)


def add_kernel(a, b, c, d, first, second):
    first[...] = (a[...].astype(F32) + b[...].astype(F32)).astype(BF16)
    second[...] = (c[...].astype(F32) + d[...].astype(F32)).astype(BF16)


def two_sums(a, b, c, d):
    shape = jax.ShapeDtypeStruct(a.shape, a.dtype)
    return pl.pallas_call(
        add_kernel,
        out_shape=[shape] * 2,
        in_specs=[in_vmem()] * 4,
        out_specs=[in_vmem()] * 2,
        cost_estimate=pl.CostEstimate(flops=a.size * 2, bytes_accessed=2_000_000, transcendentals=0),
    )(a, b, c, d)


def attend_kernel(place, starts, lengths, groups, q0, q1, q3, k0, k1, k3, *outs):
    *outs, held = outs
    heads = q0.shape[1] // HEAD
    cores, sides = 2, len(outs)
    keys = q0.shape[0] // (cores * sides)
    scale = 1.0 / math.sqrt(HEAD)
    tokens = q0.shape[0]
    square = (tokens, tokens)
    rows, columns = iota(square, 0), iota(square, 1)
    same = (
        described(rows, -1, starts, lengths, groups)[0]
        == described(columns, -2, starts, lengths, groups)[0]
    )
    keep = same | (rows == columns)
    half = HEAD // 2
    lane = iota((tokens, HEAD), 1)
    offset = described(iota((tokens, HEAD), 0), -1, starts, lengths, groups)[1]
    frequency = jnp.exp(lax.rem(lane, half).astype(F32) * (-2.0 * math.log(10000.0) / HEAD))
    angles = offset.astype(F32) * frequency
    cos = jnp.cos(angles)
    sin = jnp.where(lane < half, -jnp.sin(angles), jnp.sin(angles))

    def turned(parts, h):
        cols = pl.ds(h * HEAD, HEAD)
        own, left, right = parts
        whole = own[:, cols].astype(F32) + left[:, cols].astype(F32) + right[:, cols].astype(F32)
        return (whole * cos + pltpu.roll(whole, HEAD // 2, 1) * sin).astype(BF16)

    for h in range(heads):
        query = turned((q0, q1, q3), h)
        key = turned((k0, k1, k3), h)
        scores = (
            lax.dot_general(key, query, (((1,), (1,)), ((), ())), preferred_element_type=F32)
            * scale
        )
        masked = jnp.where(keep, scores, -1e30)
        largest = jnp.max(masked, axis=0, keepdims=True)
        powers = jnp.exp(masked - largest)
        held[...] = (powers / jnp.sum(powers, axis=0, keepdims=True)).astype(BF16)
        for side in range(sides):
            for core in range(cores):
                block = lax.rem(place[2] + side, sides) * cores + lax.rem(place[3] + core, cores)
                mine = pl.ds(pl.multiple_of(block * keys, keys), keys)
                outs[side][core, h] = held[mine, :]


def attend(place, chains, *operands):
    width, columns = operands[0].shape
    heads = columns // HEAD
    return pl.pallas_call(
        attend_kernel,
        out_shape=[jax.ShapeDtypeStruct((2, heads, width // 8, width), BF16)] * SIDE,
        in_specs=[in_smem()] * 4 + [in_vmem()] * 6,
        out_specs=[in_vmem()] * SIDE,
        scratch_shapes=[pltpu.VMEM((width, width), BF16)],
        compiler_params=pltpu.CompilerParams(vmem_limit_bytes=VMEM_LIMIT),
        cost_estimate=pl.CostEstimate(
            flops=2 * heads * HEAD * width * width,
            bytes_accessed=3_000_000,
            transcendentals=heads * width * width,
        ),
    )(place, *chains, *operands)


def older_kernel(maps, weight, *refs):
    out = refs[-1]
    turned = weight[: maps.shape[0], :].T
    by_key = jnp.swapaxes(maps[:, 0], 0, 1)
    for u in range(maps.shape[2]):
        out[u] = jnp.dot(turned, by_key[u], preferred_element_type=F32).T.astype(BF16)


def older_part(half, maps, weight, before=None):
    depth, _, keys, queries = maps.shape
    channels = weight.shape[1]
    some = keys // 2
    extra = () if before is None else (before,)
    return pl.pallas_call(
        older_kernel,
        out_shape=jax.ShapeDtypeStruct((keys, queries, channels), BF16),
        grid=(1,),
        in_specs=[
            pl.BlockSpec((depth, 1, some, queries), lambda i: (0, 0, half, 0)),
            pl.BlockSpec(weight.shape, lambda i: (0, 0)),
        ]
        + [pl.BlockSpec(memory_space=pl.ANY)] * len(extra),
        out_specs=pl.BlockSpec((some, queries, channels), lambda i: (half, 0, 0)),
        input_output_aliases={2: 0} if extra else {},
        compiler_params=pltpu.CompilerParams(vmem_limit_bytes=40 * 1024 * 1024),
        cost_estimate=pl.CostEstimate(
            flops=2 * depth * some * queries * channels,
            bytes_accessed=2 * depth * some * queries,
            transcendentals=0,
        ),
    )(maps, weight, *extra)


def described(places, outside, starts, lengths, groups):
    ids = jnp.full(places.shape, outside, jnp.int32)
    offset = jnp.zeros(places.shape, jnp.int32)
    for c in range(starts.shape[1]):
        first = starts[0, c]
        member = (places >= first) & (places < first + lengths[0, c])
        ids = jnp.where(member, groups[0, c], ids)
        offset = jnp.where(member, places - first, offset)
    return ids, offset


def iota(shape, dim):
    return lax.broadcasted_iota(jnp.int32, shape, dim)


def refine_kernel(owners, place, starts, lengths, groups, older, *refs):
    maps, refs = refs[: SIDE + 1], refs[SIDE + 1 :]
    (pair_weight, pair_bias, gain, norm_bias, hidden_weight, hidden_bias, out_weight) = refs[:7]
    out_bias, out = refs[7:9]
    (by_key, new_weight, hidden_two, out_two, ones, query_ids, key_ids) = refs[9:16]
    zeros, staged, zero_sems, tile_sems = refs[16:]
    step = pl.program_id(0)
    keys, queries, channels = older.shape
    hidden_width = hidden_bias.shape[1]
    count = out.shape[0]
    tiles = owners.shape[0]
    tile = queries // tiles

    def empty(o):
        none = owners[0] != o
        for i in range(1, tiles):
            none = none & (owners[i] != o)
        return none

    def blank(o):
        return pltpu.make_async_copy(zeros, out.at[o], zero_sems.at[o])

    def sent(r):
        some = pl.ds(pl.multiple_of(step * keys * tile, keys * tile), keys * tile)
        return pltpu.make_async_copy(
            staged.at[r, some], out.at[owners[r], some], tile_sems.at[step, r]
        )

    @pl.when(step == 0)
    def _():
        zeros[...] = jnp.zeros_like(zeros)
        for o in range(count):

            @pl.when(empty(o))
            def _(o=o):
                blank(o).start()

        parts = [m[0] for m in maps[:SIDE]] + [maps[SIDE][1 - place[3], i] for i in range(SIDE)]
        by_key[...] = jnp.swapaxes(jnp.concatenate(parts, axis=0), 0, 1)
        heads_all = by_key.shape[1]
        per_core = heads_all // (2 * SIDE)
        shape = (heads_all, heads_all)
        at = iota(shape, 1)
        piece = lax.rem(at // per_core, SIDE)
        shift = jnp.where(piece == 1, 3, jnp.where(piece == 2, 1, jnp.where(piece == 3, 2, 0)))
        core = lax.rem(at // (per_core * SIDE) + place[3], 2)
        side = lax.rem(place[2] + shift, SIDE)
        head = (side * 2 + core) * per_core + lax.rem(at, per_core)
        chosen = jnp.where(iota(shape, 0) == head, 1.0, 0.0).astype(BF16)
        old = pair_weight.shape[0] - heads_all
        new_weight[...] = lax.dot_general(
            pair_weight[old:, :], chosen, (((0,), (0,)), ((), ())), preferred_element_type=F32
        ).astype(BF16)
        query_ids[...] = described(iota(query_ids.shape, 0), -1, starts, lengths, groups)[
            0
        ].astype(F32)
        first_key = (place[2] * 2 + place[3]) * key_ids.shape[0]
        key_ids[...] = described(
            iota(key_ids.shape, 0) + first_key, -2, starts, lengths, groups
        )[0].astype(F32)
        shape = ones.shape
        ones[...] = jnp.where(
            iota(shape, 0) // channels == iota(shape, 1) // channels, 1.0, 0.0
        ).astype(BF16)
        hidden_two[...] = jnp.zeros_like(hidden_two)
        hidden_two[:channels, :hidden_width] = hidden_weight[...]
        hidden_two[channels:, hidden_width:] = hidden_weight[...]
        out_two[...] = jnp.zeros_like(out_two)
        out_two[:hidden_width, :channels] = out_weight[...]
        out_two[hidden_width:, channels:] = out_weight[...]

    twice = lambda ref: jnp.concatenate([ref[...], ref[...]], axis=1)
    gain_two, norm_two, hbias_two, obias_two = (
        twice(ref) for ref in (gain, norm_bias, hidden_bias, out_bias)
    )

    def pair_of(e):
        fresh = jnp.dot(new_weight[...], by_key[step * keys + e], preferred_element_type=F32).T
        return older[e].astype(F32) + fresh + pair_bias[...]

    span = 2 * BATCH
    for base in range(0, keys, 2 * span):
        pair = jnp.concatenate(
            [
                jnp.concatenate([pair_of(base + span * side + e) for e in range(span)], axis=0)
                for side in range(2)
            ],
            axis=1,
        ).astype(BF16)
        values = pair.astype(F32)
        mean = jnp.dot(pair, ones[...], preferred_element_type=F32) * (1.0 / channels)
        centred = values - mean
        spread = jnp.dot(
            (centred * centred).astype(BF16), ones[...], preferred_element_type=F32
        ) * (1.0 / channels)
        normed = (centred * lax.rsqrt(spread + 1e-05) * gain_two + norm_two).astype(BF16)
        hidden = jnp.maximum(
            jnp.dot(normed, hidden_two[...], preferred_element_type=F32) + hbias_two, 0.0
        ).astype(BF16)
        update = jnp.dot(hidden, out_two[...], preferred_element_type=F32) + obias_two
        result = values + update
        for side in range(2):
            for e in range(span):
                u = step * keys + base + span * side + e
                piece = result[
                    e * queries : (e + 1) * queries, side * channels : (side + 1) * channels
                ]
                same = key_ids[pl.ds(u, 1), :] == query_ids[...]
                piece = jnp.where(same, piece, 0.0).astype(BF16)
                at = pl.ds(pl.multiple_of(u * tile, tile), tile)
                for r in range(tiles):
                    staged[r, at, :] = piece[r * tile : (r + 1) * tile]

    for r in range(tiles):

        @pl.when(owners[r] >= 0)
        def _(r=r):
            sent(r).start()

    @pl.when(step == pl.num_programs(0) - 1)
    def _():
        for r in range(tiles):

            @pl.when(owners[r] >= 0)
            def _(r=r):
                for s in range(STEPS):
                    some = pl.ds(s * keys * tile, keys * tile)
                    pltpu.make_async_copy(
                        staged.at[r, some], out.at[owners[r], some], tile_sems.at[s, r]
                    ).wait()

        for o in range(count):

            @pl.when(empty(o))
            def _(o=o):
                blank(o).wait()


def refine(owners, count, place, chains, older, maps, weights):
    keys, queries, channels = older.shape
    tiles = owners.shape[0]
    tile_pairs = keys * queries // tiles
    hidden = weights[4].shape[1]
    heads_all = 2 * SIDE * maps[0].shape[1]
    whole = lambda a: pl.BlockSpec(a.shape, lambda i, n=a.ndim: (0,) * n)
    return pl.pallas_call(
        refine_kernel,
        out_shape=jax.ShapeDtypeStruct((count, tile_pairs, channels), BF16),
        grid=(STEPS,),
        in_specs=[in_smem()] * 5
        + [pl.BlockSpec((keys // STEPS, queries, channels), lambda i: (i, 0, 0))]
        + [whole(a) for a in (*maps, *weights)],
        out_specs=pl.BlockSpec(memory_space=pl.ANY),
        scratch_shapes=[
            pltpu.VMEM((keys, heads_all, queries), BF16),
            pltpu.VMEM((channels, heads_all), BF16),
            pltpu.VMEM((2 * channels, 2 * hidden), BF16),
            pltpu.VMEM((2 * hidden, 2 * channels), BF16),
            pltpu.VMEM((2 * channels, 2 * channels), BF16),
            pltpu.VMEM((queries, channels), F32),
            pltpu.VMEM((keys, channels), F32),
            pltpu.VMEM((tile_pairs, channels), BF16),
            pltpu.VMEM((tiles, tile_pairs, channels), BF16),
            pltpu.SemaphoreType.DMA((count,)),
            pltpu.SemaphoreType.DMA((STEPS, tiles)),
        ],
        compiler_params=pltpu.CompilerParams(vmem_limit_bytes=VMEM_LIMIT),
        cost_estimate=pl.CostEstimate(
            flops=4 * keys * queries * channels * 640,
            bytes_accessed=10_000_000,
            transcendentals=0,
        ),
    )(owners, place, *chains, older, *maps, *weights)


def body(
    tokens,
    query_weight,
    key_weight,
    old_maps,
    pair_weight,
    pair_bias,
    norm_gain,
    norm_bias,
    hidden_weight,
    hidden_bias,
    out_weight,
    out_bias,
    chain_starts,
    chain_lengths,
    chain_groups,
    tile_owner,
):
    row_count = lax.axis_size(DP)
    bin_tokens = tokens.shape[0]
    place = jnp.stack([lax.axis_index(a) for a in ("x", "z", "y", "k")])
    place = place.astype(jnp.int32)

    q_left, q_right = gathered_rows(query_weight)
    k_left, k_right = gathered_rows(key_weight)
    older = older_part(0, old_maps, pair_weight)
    q_left, k_right, older = lax.optimization_barrier((q_left, k_right, older))
    q_far = shifted(q_left, "x", 1)
    k_far = shifted(k_right, "x", -1)
    blocks = token_blocks(tokens)
    older = older_part(1, old_maps, pair_weight, older)
    blocks, older = lax.optimization_barrier((blocks, older))
    tok = turn(place, blocks)
    partial = project(
        tok, (query_weight, q_left, q_right, q_far, key_weight, k_left, k_right, k_far)
    )
    chains = (chain_starts, chain_lengths, chain_groups)
    row = lambda a: a.reshape(1, -1)
    q_zero, k_zero, q_one, k_one, q_three, k_three, q_two, k_two = (
        partial[i] for i in (0, 1, 2, 3, 6, 7, 4, 5)
    )
    q_two = shifted(q_two, "z", 1)
    k_two = shifted(k_two, "z", -1)
    k_one = shifted(k_one, "z", 1)
    q_three = shifted(q_three, "z", -1)
    q_one, k_three = two_sums(q_one, q_two, k_three, k_two)
    q_one = shifted(q_one, "z", 1)
    k_three = shifted(k_three, "z", -1)

    maps = attend(place, chains, q_zero, q_one, q_three, k_zero, k_one, k_three)
    pieces = [maps[0]] + [shifted(maps[by % SIDE], "y", by) for by in (1, -1, 2)]
    both = lax.all_gather(jnp.stack([p[1] for p in pieces]), "k")
    outgoing = refine(
        tile_owner[0, 0],
        row_count,
        place,
        chains,
        older,
        (*pieces, both),
        (
            pair_weight,
            row(pair_bias),
            row(norm_gain),
            row(norm_bias),
            hidden_weight,
            row(hidden_bias),
            out_weight,
            row(out_bias),
        ),
    )
    outgoing = outgoing.reshape(1, row_count, 1, *outgoing.shape[1:])
    return lax.all_to_all(outgoing, DP, split_axis=1, concat_axis=1, tiled=True)


def solution(mesh):
    split = Mesh(mesh.devices.reshape(SIDE, SIDE, SIDE, 2), ("x", "z", "y", "k"))
    placed = (
        P(DP, COL),
        P(DP, COL),
        P(DP, COL),
        P(None, DP, COL, None),
        P(),
        P(),
        P(),
        P(),
        P(),
        P(),
        P(),
        P(),
        P(DP, None),
        P(DP, None),
        P(DP, None),
        P(DP, COL, None),
    )
    return jax.shard_map(
        body, mesh=split, in_specs=placed, out_specs=P(DP, None, COL, None, None), check_vma=False
    )
```
